32 devices in a mesh: dp: 4 (over y, x), lat: 2 (over core), lon: 4 (over z).
Axes of the slice: x: 2, y: 2, z: 4, core: 2. Of those that a mesh axis runs over, the one named last changes fastest.
Arguments:
- tokens: bfloat16 [4, 3, 12, 48, 1024], P('dp', None, 'lat', 'lon'), may hold values from -6 to 6
- cotangent: bfloat16 [4, 3, 12, 48, 1024], P('dp', None, 'lat', 'lon'), may hold values from -6 to 6
- w_qkv: bfloat16 [2, 1024, 1536], P(None, ('lat', 'lon')), may hold values from -0.25 to 0.25
- w_out: bfloat16 [2, 512, 1024], P(None, ('lat', 'lon')), may hold values from -0.25 to 0.25
- gains: float32 [2, 1024], replicated, may hold values from 0.1 to 1.9
- tables: float32 [2, 8, 1265], replicated, may hold values from -8 to 304
Outputs:
- outputs: bfloat16 [4, 3, 12, 48, 1024], P('dp', None, 'lat', 'lon')
- grad_tokens: bfloat16 [4, 3, 12, 48, 1024], P('dp', None, 'lat', 'lon')
- grad_gains: float32 [2, 1024], replicated
- grad_tables: float32 [2, 8, 1265], replicated
The draws below stay inside these ranges and needn't reach their ends.
All inputs are finite; a program needn't handle non-finite values.
Results may differ from the reference program's by a relative error of at most 0.033.
Values may be sent and summed in bfloat16 or wider, within the bound.
A program may use at most 128 MiB of HBM per device.

```python
import math
import jax
import jax.numpy as jnp
from jax import lax

D = 1024
HD = 64
H = 8
Z = 3
WH = 6
WW = 12
SH = 3
SW = 6
RELS = 1265
TIMES = 4
NH = 12
NW = 48


def draw_tables(key, part):
    key = jax.random.fold_in(key, 11)
    shape = (2, H, RELS)
    return jnp.clip(2.0 * jax.random.normal(key, shape, jnp.float32), -8.0, 8.0)


def level_of(own_key, dims, split, low, top_value):
    level = 1.0
    for position, blocks in split:
        heights = jax.random.uniform(jax.random.fold_in(jax.random.fold_in(own_key, 6), position), (blocks,), jnp.float32, low / len(split), top_value / len(split))
        level = level * jnp.repeat(jnp.exp(heights), dims[position] // blocks).reshape((-1,) + (1,) * (len(dims) - 1 - position))
    return level


def normal_values(rng, dims, deviation, reach, shards=(), held_as=jnp.bfloat16):
    drawn = jax.random.normal(rng, dims, jnp.float32) * deviation
    if len(shards) > 0:
        drawn = level_of(rng, dims, shards, -0.22, 0.18) * drawn
    return jnp.clip(drawn, min=-reach, max=reach).astype(held_as)


def setup_inputs(seed: int = 0) -> dict:
    arg_keys = jax.random.split(jax.random.key(seed), 7)
    tokens = normal_values(arg_keys[0], (TIMES, Z, NH, NW, D), 1.0, 6.0, ((0, 4), (2, 2), (3, 4)))
    cotangent = normal_values(arg_keys[1], (TIMES, Z, NH, NW, D), 1.0, 6.0, ((0, 4), (2, 2), (3, 4)))
    w_qkv = normal_values(arg_keys[2], (2, D, 3 * H * HD), (D // 2) ** -0.5, 0.25, ((1, 8),))
    w_out = normal_values(arg_keys[3], (2, H * HD, D), (H * HD) ** -0.5, 0.25, ((1, 8),))
    gains = jnp.clip(1.0 + 0.18 * jax.random.normal(arg_keys[4], (2, D), jnp.float32), 0.1, 1.9)
    tables = draw_tables(jax.random.fold_in(arg_keys[6], 71), 0)
    return dict(tokens=tokens, cotangent=cotangent, w_qkv=w_qkv, w_out=w_out, gains=gains, tables=tables)


EPS = 1e-05
HIGH = lax.Precision.HIGHEST

def widened(array):
    return lax.optimization_barrier(array).astype(jnp.float32)

def offset_table():
    shape = (Z, WH, WW)
    level_ids = lax.broadcasted_iota(jnp.int32, shape, 0).reshape(-1)
    row_ids = lax.broadcasted_iota(jnp.int32, shape, 1).reshape(-1)
    col_ids = lax.broadcasted_iota(jnp.int32, shape, 2).reshape(-1)
    delta_z = level_ids[:, None] - level_ids[None, :]
    delta_y = row_ids[:, None] - row_ids[None, :]
    delta_x = col_ids[:, None] - col_ids[None, :]
    flat = (delta_z + Z - 1) * (2 * WH - 1) * (2 * WW - 1) + (delta_y + WH - 1) * (2 * WW - 1) + delta_x + WW - 1
    return flat.astype(jnp.int32)

def to_windows(grid):
    time_count, levels, lat_rows, lon_cols, features = grid.shape
    grid = grid.reshape(time_count, levels, lat_rows // WH, WH, lon_cols // WW, WW, features)
    grid = grid.transpose(0, 2, 4, 1, 3, 5, 6)
    return grid.reshape(time_count * (lat_rows // WH) * (lon_cols // WW), levels * WH * WW, features)

def from_windows(windows, time_count, lat_rows, lon_cols):
    features = windows.shape[-1]
    grid = windows.reshape(time_count, lat_rows // WH, lon_cols // WW, Z, WH, WW, features)
    grid = grid.transpose(0, 3, 1, 4, 2, 5, 6)
    return grid.reshape(time_count, Z, lat_rows, lon_cols, features)

def region_pairs(region):
    labels = to_windows(region[None, :, :, :, None])[:, :, 0]
    return labels[:, :, None] == labels[:, None, :]

def norm_parts(field, gain):
    values = field.astype(jnp.float32)
    centred = values - lax.optimization_barrier(jnp.mean(values, -1, keepdims=True))
    inverse = lax.rsqrt(lax.optimization_barrier(jnp.mean(centred * centred, -1, keepdims=True)) + EPS)
    normed = centred * inverse
    return ((normed * gain).astype(jnp.bfloat16), normed, inverse)

def block_forward(field, gain, w_in, w_proj, bias, valid):
    time_count, levels, lat_rows, lon_cols, features = field.shape
    scale = HD ** (-0.5)
    normed_bf, normed, inverse = norm_parts(field, gain)
    mixed = jnp.dot(normed_bf.reshape(-1, features), w_in, preferred_element_type=jnp.float32).astype(jnp.bfloat16)
    windows = to_windows(mixed.reshape(time_count, levels, lat_rows, lon_cols, 3 * H * HD))
    parts = widened(windows).reshape(windows.shape[0], windows.shape[1], 3, H, HD)
    query, keys, values = (parts[:, :, 0], parts[:, :, 1], parts[:, :, 2])
    scores = jnp.einsum('nihd,njhd->nhij', query, keys, precision=HIGH) * scale + bias[None]
    scores = jnp.where(valid[:, None], scores, -1e+30)
    powers = jnp.exp(scores - lax.optimization_barrier(jnp.max(scores, -1, keepdims=True)))
    probs = (powers / lax.optimization_barrier(jnp.sum(powers, -1, keepdims=True))).astype(jnp.bfloat16)
    context = jnp.einsum('nhij,njhd->nihd', widened(probs), values, precision=HIGH).astype(jnp.bfloat16)
    context = from_windows(context.reshape(windows.shape[0], windows.shape[1], H * HD), time_count, lat_rows, lon_cols)
    branch = jnp.dot(context.reshape(-1, H * HD), w_proj, preferred_element_type=jnp.float32)
    result = (field.astype(jnp.float32) + branch.reshape(field.shape)).astype(jnp.bfloat16)
    return (result, (normed, inverse, windows, probs))

def block_backward(grad_out, saved, gain, w_in, w_proj):
    normed, inverse, windows, probs = saved
    time_count, levels, lat_rows, lon_cols, features = grad_out.shape
    scale = HD ** (-0.5)
    flat = grad_out.reshape(-1, features)
    grad_ctx = lax.dot_general(flat, w_proj, (((1,), (1,)), ((), ())), preferred_element_type=jnp.float32).astype(jnp.bfloat16)
    grad_win = to_windows(grad_ctx.reshape(time_count, levels, lat_rows, lon_cols, H * HD))
    count, span = (grad_win.shape[0], grad_win.shape[1])
    grad_win = widened(grad_win).reshape(count, span, H, HD)
    parts = widened(windows).reshape(count, span, 3, H, HD)
    query, keys, values = (parts[:, :, 0], parts[:, :, 1], parts[:, :, 2])
    weights = widened(probs)
    grad_probs = jnp.einsum('nihd,njhd->nhij', grad_win, values, precision=HIGH)
    grad_scores = weights * (grad_probs - lax.optimization_barrier(jnp.sum(grad_probs * weights, -1, keepdims=True)))
    bias_term = lax.optimization_barrier(jnp.sum(grad_scores, 0))
    scores_bf = widened(grad_scores.astype(jnp.bfloat16))
    grad_query = (jnp.einsum('nhij,njhd->nihd', scores_bf, keys, precision=HIGH) * scale).astype(jnp.bfloat16)
    grad_keys = (jnp.einsum('nhij,nihd->njhd', scores_bf, query, precision=HIGH) * scale).astype(jnp.bfloat16)
    grad_values = jnp.einsum('nhij,nihd->njhd', weights, grad_win, precision=HIGH).astype(jnp.bfloat16)
    grad_mixed = jnp.stack([grad_query, grad_keys, grad_values], 2).reshape(count, span, 3 * H * HD)
    grad_grid = from_windows(grad_mixed, time_count, lat_rows, lon_cols).reshape(-1, 3 * H * HD)
    grad_norm = lax.dot_general(grad_grid, w_in, (((1,), (1,)), ((), ())), preferred_element_type=jnp.float32)
    flat_normed = normed.reshape(-1, features)
    flat_inverse = inverse.reshape(-1, 1)
    gain_term = lax.optimization_barrier(jnp.sum(grad_norm * flat_normed, 0))
    scaled = grad_norm * gain
    grad_field = flat_inverse * (scaled - lax.optimization_barrier(jnp.mean(scaled, -1, keepdims=True)) - flat_normed * lax.optimization_barrier(jnp.mean(scaled * flat_normed, -1, keepdims=True)))
    grad_in = (flat.astype(jnp.float32) + grad_field).astype(jnp.bfloat16).reshape(grad_out.shape)
    return (grad_in, gain_term, bias_term)

def reference(tokens, cotangent, w_qkv, w_out, gains, tables):
    offsets = offset_table()
    bias_one = tables[0][:, offsets]
    bias_two = tables[1][:, offsets]
    row_ids = lax.broadcasted_iota(jnp.int32, (Z, NH, NW), 1)
    region = jnp.where(row_ids >= NH - SH, 1, 0).astype(jnp.int32)
    valid_two = region_pairs(region)
    valid_one = jnp.ones(valid_two.shape, jnp.bool_)

    def one_time(pair):
        field = pair[0][None]
        seed_grad = pair[1][None]
        first, saved_one = block_forward(field, gains[0], w_qkv[0], w_out[0], bias_one, valid_one)
        rolled = jnp.roll(first, (-SH, -SW), (2, 3))
        second, saved_two = block_forward(rolled, gains[1], w_qkv[1], w_out[1], bias_two, valid_two)
        result = jnp.roll(second, (SH, SW), (2, 3))
        grad_two, gain_two, table_two = block_backward(jnp.roll(seed_grad, (-SH, -SW), (2, 3)), saved_two, gains[1], w_qkv[1], w_out[1])
        grad_one, gain_one, table_one = block_backward(jnp.roll(grad_two, (SH, SW), (2, 3)), saved_one, gains[0], w_qkv[0], w_out[0])
        return (result[0], grad_one[0], jnp.stack([gain_one, gain_two]), jnp.stack([table_one, table_two]))
    results, grads, gain_terms, table_terms = lax.map(one_time, (tokens, cotangent))
    norm_scale = 1.0 / math.sqrt(TIMES * Z * NH * NW)
    grad_gains = lax.optimization_barrier(jnp.sum(gain_terms, 0)) * norm_scale
    summed = lax.optimization_barrier(jnp.sum(table_terms, 0)).reshape(2 * H, -1)
    folded = jax.ops.segment_sum(summed.T, offsets.reshape(-1).astype(jnp.int32), num_segments=RELS).T
    grad_tables = folded.reshape(2, H, RELS) * norm_scale
    return (results, grads, grad_gains, grad_tables)
```

```python
import functools
import math

import jax
import jax.numpy as jnp
import numpy as np
from jax import lax
from jax.experimental import pallas as pl
from jax.experimental.pallas import tpu as pltpu
from jax.sharding import PartitionSpec as P

MESH = pl.DeviceIdType.MESH
HD = 64
H = 8
Z = 3
WH = 6
WW = 12
SH = 3
SW = 6
EPS = 1e-05
RELS = (2 * Z - 1) * (2 * WH - 1) * (2 * WW - 1)
STEP_Z = (2 * WH - 1) * (2 * WW - 1)
STEP_Y = 2 * WW - 1
CENTRE = (Z - 1) * STEP_Z + (WH - 1) * STEP_Y + WW - 1
QR = 64
ROWS = 4 * QR
SPAN = 640
TABLE = 1280
GROUPS = Z * SH
LINES = Z * WH
LINE = 16
SCALE = HD ** (-0.5)
FAR = -1e30
VMEM_LIMIT = 58 * 1024 * 1024


def token_places():
    places = []
    for row in range(ROWS):
        quad, inner = divmod(row, QR)
        if inner >= GROUPS * SW:
            places.append(None)
            continue
        group, x = divmod(inner, SW)
        z, y = divmod(group, SH)
        places.append((z, y + SH * (quad // 2), x + SW * (quad % 2)))
    return places


def order_matrix():
    order = np.zeros((ROWS, LINES * LINE), np.float32)
    for row, place in enumerate(token_places()):
        if place is not None:
            z, y, x = place
            order[row, (z * WH + y) * LINE + x] = 1
    return order


def spread_matrix():
    spread = np.zeros((SPAN, ROWS), np.float32)
    for row, place in enumerate(token_places()):
        if place is not None:
            z, y, x = place
            spread[z * STEP_Z + y * STEP_Y + x, row] = 1
    return spread


def group_list():
    groups = []
    for quad in range(4):
        for group in range(GROUPS):
            z, y = divmod(group, SH)
            start = z * STEP_Z + (y + SH * (quad // 2)) * STEP_Y + SW * (quad % 2)
            groups.append((quad * QR + group * SW, CENTRE - start))
    return groups


def dot(a, b):
    return jnp.dot(a, b, preferred_element_type=jnp.float32)


def dot_t(a, b):
    return lax.dot_general(a, b, (((1,), (1,)), ((), ())), preferred_element_type=jnp.float32)


def t_dot(a, b):
    return lax.dot_general(a, b, (((0,), (0,)), ((), ())), preferred_element_type=jnp.float32)


def prep_kernel(tok, cot, tab, order, spread, flag, x_out, g_out, bias_out, lines, rows):
    lines[...] = jnp.zeros_like(lines)
    for source, target in ((tok, x_out), (cot, g_out)):
        for k in range(LINES):
            lines[k, 0:WW, :] = source[k // WH, k % WH]
        flat = lines[...].reshape(LINES * LINE, lines.shape[2])
        target[...] = dot(order[...], flat).astype(jnp.bfloat16)
    rows[...] = jnp.zeros_like(rows)
    key = lax.broadcasted_iota(jnp.int32, (ROWS, ROWS), 1)
    query = lax.broadcasted_iota(jnp.int32, (ROWS, ROWS), 0)
    pad = key % QR >= GROUPS * SW
    apart = (key // (2 * QR)) != (query // (2 * QR))
    drop_two = pad | (apart & (flag[0] == 1))

    def one_head(n, carry):
        base = jnp.broadcast_to(tab[n], (8, TABLE))
        base = pltpu.roll(base, 0, 1, stride=1, stride_axis=0)
        for row, shift in group_list():
            rows[row : row + SW, :] = pltpu.roll(base, TABLE - shift, 1)[:SW, :SPAN]
        wide = rows[...]
        high = wide.astype(jnp.bfloat16)
        rest = wide - high.astype(jnp.float32)
        mid = rest.astype(jnp.bfloat16)
        low = (rest - mid.astype(jnp.float32)).astype(jnp.bfloat16)
        part = spread[...]
        bias = dot(high, part) + dot(mid, part) + dot(low, part)
        bias_out[n] = bias
        return carry

    lax.fori_loop(0, 2 * H, one_head, 0)

    def mask_head(n, carry):
        bias_out[n] = jnp.where(pad, FAR, bias_out[n])
        bias_out[n + H] = jnp.where(drop_two, FAR, bias_out[n + H])
        return carry

    lax.fori_loop(0, H, mask_head, 0)


def normalise(values):
    centred = values - jnp.mean(values, -1, keepdims=True)
    inverse = lax.rsqrt(jnp.mean(centred * centred, -1, keepdims=True) + EPS)
    return centred * inverse, inverse


def half_mask(which):
    lane = lax.broadcasted_iota(jnp.int32, (ROWS, 2 * HD), 1)
    return (lane // HD) == which


def forward_kernel(x_ref, gain, w_in, w_proj, bias, y_out, qkv, probs, ctx):
    normed, _ = normalise(x_ref[...].astype(jnp.float32))
    qkv[...] = dot((normed * gain[...]).astype(jnp.bfloat16), w_in[...]).astype(jnp.bfloat16)
    first_half = half_mask(0)
    for pair in range(H // 2):
        lo, hi = pair * 2 * HD, (pair + 1) * 2 * HD
        query = qkv[:, lo:hi] * jnp.bfloat16(SCALE)
        keys = qkv[:, H * HD + lo : H * HD + hi]
        values = qkv[:, 2 * H * HD + lo : 2 * H * HD + hi]
        found = []
        for side in range(2):
            keep = first_half if side == 0 else ~first_half
            scores = dot_t(jnp.where(keep, query, 0), keys) + bias[2 * pair + side]
            powers = jnp.exp(scores - jnp.max(scores, -1, keepdims=True))
            weights = (powers / jnp.sum(powers, -1, keepdims=True)).astype(jnp.bfloat16)
            probs[2 * pair + side] = weights
            found.append(dot(weights, values))
        ctx[:, lo:hi] = jnp.where(first_half, found[0], found[1]).astype(jnp.bfloat16)
    y_out[...] = (x_ref[...].astype(jnp.float32) + dot(ctx[...], w_proj[...])).astype(jnp.bfloat16)


def backward_core(g_ref, x_ref, gain, w_in, w_proj, qkv, probs, collect, gain_out, table_out,
                  gctx, gqkv, wide):
    gctx[...] = dot_t(g_ref[...], w_proj[...]).astype(jnp.bfloat16)
    first_half = half_mask(0)
    row_in_group = lax.broadcasted_iota(jnp.int32, (8, SPAN), 0) < SW
    zeros = jnp.zeros((8, TABLE - SPAN), jnp.float32)
    for pair in range(H // 2):
        lo, hi = pair * 2 * HD, (pair + 1) * 2 * HD
        query = qkv[:, lo:hi]
        keys = qkv[:, H * HD + lo : H * HD + hi]
        values = qkv[:, 2 * H * HD + lo : 2 * H * HD + hi]
        part = gctx[:, lo:hi]
        grads = []
        for side in range(2):
            head = 2 * pair + side
            keep = first_half if side == 0 else ~first_half
            weights_bf = probs[head]
            weights = weights_bf.astype(jnp.float32)
            grad_probs = dot_t(jnp.where(keep, part, 0), values)
            grad_scores = weights * (
                grad_probs - jnp.sum(grad_probs * weights, -1, keepdims=True)
            )
            s = grad_scores.astype(jnp.bfloat16)
            rest = (grad_scores - s.astype(jnp.float32)).astype(jnp.bfloat16)
            wide[head] = dot(s, collect[...]) + dot(rest, collect[...])
            grads.append((dot(s, keys), t_dot(s, query), t_dot(weights_bf, part)))
        for which, factor in ((0, SCALE), (1, SCALE), (2, 1.0)):
            both = jnp.where(first_half, grads[0][which], grads[1][which]) * factor
            at = which * H * HD
            gqkv[:, at + lo : at + hi] = both.astype(jnp.bfloat16)

    def fold(head, carry):
        total = jnp.zeros((8, TABLE), jnp.float32)
        for row, shift in group_list():
            rows = jnp.where(row_in_group, wide[head, row : row + 8, :], 0.0)
            total = total + pltpu.roll(jnp.concatenate([rows, zeros], 1), shift, 1)
        line = total[0:1]
        for x in range(1, SW):
            line = line + pltpu.roll(total[x : x + 1], TABLE - x, 1)
        table_out[head] = line
        return carry

    lax.fori_loop(0, H, fold, 0)
    grad_u = dot_t(gqkv[...], w_in[...])
    normed, inverse = normalise(x_ref[...].astype(jnp.float32))
    gain_out[...] = jnp.sum(grad_u * normed, 0, keepdims=True)
    scaled = grad_u * gain[...]
    return g_ref[...].astype(jnp.float32) + inverse * (
        scaled
        - jnp.mean(scaled, -1, keepdims=True)
        - normed * jnp.mean(scaled * normed, -1, keepdims=True)
    )


def backward_kernel(g_ref, x_ref, gain, w_in, w_proj, qkv, probs, collect,
                    gx_out, gain_out, table_out, gctx, gqkv, wide):
    grad = backward_core(g_ref, x_ref, gain, w_in, w_proj, qkv, probs, collect, gain_out,
                         table_out, gctx, gqkv, wide)
    gx_out[...] = grad.astype(jnp.bfloat16)


def last_kernel(g_ref, x_ref, gain, w_in, w_proj, qkv, probs, collect, y_ref, order,
                gx_out, gain_out, table_out, y_out, gctx, gqkv, wide):
    grad = backward_core(g_ref, x_ref, gain, w_in, w_proj, qkv, probs, collect, gain_out,
                         table_out, gctx, gqkv, wide)
    for source, target in ((grad.astype(jnp.bfloat16), gx_out), (y_ref[...], y_out)):
        lines = t_dot(order[...], source).astype(jnp.bfloat16)
        for k in range(LINES):
            target[k // WH, k % WH] = lines[k * LINE : k * LINE + WW]


def exchange_kernel(ahead, src, dst, send, recv, own):
    lat, lon = lax.axis_index("lat"), lax.axis_index("lon")
    lats, lons = lax.axis_size("lat"), lax.axis_size("lon")

    def to(quad, sign):
        y, x = quad // 2, quad % 2
        if ahead:
            dy, dx = 1 - y, 1 - x
        else:
            dy, dx = y, x
        return {
            "lat": lax.rem(lat + lats + sign * dy, lats),
            "lon": lax.rem(lon + lons + sign * dx, lons),
        }

    sign = -1 if ahead else 1
    moving = [quad for quad in range(4) if quad != (3 if ahead else 0)]
    barrier = pltpu.get_barrier_semaphore()
    for quad in moving:
        pl.semaphore_signal(barrier, inc=1, device_id=to(quad, -sign), device_id_type=MESH)
    stay = 3 if ahead else 0
    local = pltpu.make_async_copy(src.at[stay], dst.at[3 - stay], own)
    local.start()
    pl.semaphore_wait(barrier, 3)
    copies = []
    for n, quad in enumerate(moving):
        copies.append(
            pltpu.make_async_remote_copy(
                src_ref=src.at[quad],
                dst_ref=dst.at[3 - quad],
                send_sem=send.at[n],
                recv_sem=recv.at[n],
                device_id=to(quad, sign),
                device_id_type=MESH,
            )
        )
        copies[-1].start()
    local.wait()
    for copy in copies:
        copy.wait()


def exchange(field, ahead, number):
    quads = field.reshape(4, QR, field.shape[-1])
    moved = pl.pallas_call(
        functools.partial(exchange_kernel, ahead),
        out_shape=jax.ShapeDtypeStruct(quads.shape, quads.dtype),
        in_specs=[pl.BlockSpec(memory_space=pltpu.VMEM)],
        out_specs=pl.BlockSpec(memory_space=pltpu.VMEM),
        scratch_shapes=[
            pltpu.SemaphoreType.DMA((3,)),
            pltpu.SemaphoreType.DMA((3,)),
            pltpu.SemaphoreType.DMA,
        ],
        compiler_params=pltpu.CompilerParams(collective_id=number, has_side_effects=True),
    )(quads)
    return moved.reshape(field.shape)


def call(kernel, out, scratch, args, smem=(), flops=10**9):
    specs = [
        pl.BlockSpec(memory_space=pltpu.SMEM if n in smem else pltpu.VMEM)
        for n in range(len(args))
    ]
    return pl.pallas_call(
        kernel,
        out_shape=[jax.ShapeDtypeStruct(shape, dtype) for shape, dtype in out],
        in_specs=specs,
        out_specs=[pl.BlockSpec(memory_space=pltpu.VMEM) for _ in out],
        scratch_shapes=[pltpu.VMEM(shape, dtype) for shape, dtype in scratch],
        compiler_params=pltpu.CompilerParams(vmem_limit_bytes=VMEM_LIMIT),
        cost_estimate=pl.CostEstimate(flops=flops, bytes_accessed=8 * 2**20, transcendentals=0),
    )(*args)


def fetch_block(w_qkv, w_out, index):
    return (
        lax.all_gather(w_qkv[index], ("lat", "lon"), axis=0, tiled=True),
        lax.all_gather(w_out[index], ("lat", "lon"), axis=0, tiled=True),
    )


def on_device(tokens, cotangent, w_qkv, w_out, gains, tables):
    features = tokens.shape[-1]
    bf, f32 = jnp.bfloat16, jnp.float32
    inner = H * HD
    order = jnp.asarray(order_matrix(), bf)
    spread = jnp.asarray(spread_matrix(), bf)
    collect = jnp.asarray(spread_matrix().T.copy(), bf)
    in_one, proj_one = fetch_block(w_qkv, w_out, 0)
    in_two, proj_two = fetch_block(w_qkv, w_out, 1)
    polar = lax.axis_index("lat") == lax.axis_size("lat") - 1
    flag = jnp.where(polar, 1, 0).astype(jnp.int32).reshape(1)
    lines = jnp.pad(tables.reshape(2 * H, 1, RELS)[:, :, ::-1], ((0, 0), (0, 0), (0, TABLE - RELS)))
    field = ((ROWS, features), bf)
    x_one, g_out, bias = call(
        prep_kernel,
        [field, field, ((2 * H, ROWS, ROWS), f32)],
        [((LINES, LINE, features), bf), ((ROWS, SPAN), f32)],
        (tokens[0], cotangent[0], lines, order, spread, flag),
        smem=(5,),
        flops=8 * 10**9,
    )
    saved = [((ROWS, 3 * inner), bf), ((H, ROWS, ROWS), bf)]
    wide = [((ROWS, inner), bf)]
    g_two = exchange(g_out, True, 0)
    gain_one, gain_two = gains[0:1], gains[1:2]
    first, qkv_one, probs_one = call(
        forward_kernel, [field] + saved, wide, (x_one, gain_one, in_one, proj_one, bias[:H])
    )
    x_two = exchange(first, True, 1)
    second, qkv_two, probs_two = call(
        forward_kernel, [field] + saved, wide, (x_two, gain_two, in_two, proj_two, bias[H:])
    )
    y_back = exchange(second, False, 2)
    back = [((ROWS, inner), bf), ((ROWS, 3 * inner), bf), ((H, ROWS, SPAN), f32)]
    terms = [((1, features), f32), ((H, 1, TABLE), f32)]
    gx_two, gterm_two, tterm_two = call(
        backward_kernel,
        [field] + terms,
        back,
        (g_two, x_two, gain_two, in_two, proj_two, qkv_two, probs_two, collect),
    )
    g_one = exchange(gx_two, False, 3)
    window = (tokens.shape[1:], bf)
    grad_tokens, gterm_one, tterm_one, outputs = call(
        last_kernel,
        [window] + terms + [window],
        back,
        (g_one, x_one, gain_one, in_one, proj_one, qkv_one, probs_one, collect, y_back, order),
    )
    packed = jnp.concatenate(
        [gterm_one, gterm_two, tterm_one.reshape(1, -1), tterm_two.reshape(1, -1)], 1
    )
    packed = lax.psum(packed, ("dp", "lat", "lon"))
    total = math.prod(tokens.shape[:4]) * math.prod(
        lax.axis_size(axis) for axis in ("dp", "lat", "lon")
    )
    packed = packed * (1.0 / math.sqrt(total))
    grad_gains = packed[:, : 2 * features].reshape(2, features)
    folded = packed[:, 2 * features :].reshape(2, H, TABLE)
    grad_tables = folded[:, :, :RELS][:, :, ::-1]
    return (outputs[None], grad_tokens[None], grad_gains, grad_tables)


def solution(mesh):
    return jax.shard_map(
        on_device,
        mesh=mesh,
        in_specs=(
            P("dp", None, "lat", "lon", None),
            P("dp", None, "lat", "lon", None),
            P(None, ("lat", "lon"), None),
            P(None, ("lat", "lon"), None),
            P(),
            P(),
        ),
        out_specs=(P("dp", None, "lat", "lon", None), P("dp", None, "lat", "lon", None), P(), P()),
        check_vma=False,
    )
```

```python
import functools
import math

import jax
import jax.numpy as jnp
import numpy as np
from jax import lax
from jax.experimental import pallas as pl
from jax.experimental.pallas import tpu as pltpu
from jax.sharding import PartitionSpec as P

MESH = pl.DeviceIdType.MESH
HD = 64
H = 8
Z = 3
WH = 6
WW = 12
SH = 3
SW = 6
EPS = 1e-05
RELS = (2 * Z - 1) * (2 * WH - 1) * (2 * WW - 1)
STEP_Z = (2 * WH - 1) * (2 * WW - 1)
STEP_Y = 2 * WW - 1
CENTRE = (Z - 1) * STEP_Z + (WH - 1) * STEP_Y + WW - 1
QR = 64
ROWS = 4 * QR
SPAN = 640
TABLE = 1280
GROUPS = Z * SH
LINES = Z * WH
LINE = 16
SCALE = HD ** (-0.5)
FAR = -1e30
VMEM_LIMIT = 58 * 1024 * 1024


def token_places():
    places = []
    for row in range(ROWS):
        quad, inner = divmod(row, QR)
        if inner >= GROUPS * SW:
            places.append(None)
            continue
        group, x = divmod(inner, SW)
        z, y = divmod(group, SH)
        places.append((z, y + SH * (quad // 2), x + SW * (quad % 2)))
    return places


def order_matrix():
    order = np.zeros((ROWS, LINES * LINE), np.float32)
    for row, place in enumerate(token_places()):
        if place is not None:
            z, y, x = place
            order[row, (z * WH + y) * LINE + x] = 1
    return order


def spread_matrix():
    spread = np.zeros((SPAN, ROWS), np.float32)
    for row, place in enumerate(token_places()):
        if place is not None:
            z, y, x = place
            spread[z * STEP_Z + y * STEP_Y + x, row] = 1
    return spread


def group_list():
    groups = []
    for quad in range(4):
        for group in range(GROUPS):
            z, y = divmod(group, SH)
            start = z * STEP_Z + (y + SH * (quad // 2)) * STEP_Y + SW * (quad % 2)
            groups.append((quad * QR + group * SW, CENTRE - start))
    return groups


def dot(a, b):
    return jnp.dot(a, b, preferred_element_type=jnp.float32)


def dot_t(a, b):
    return lax.dot_general(a, b, (((1,), (1,)), ((), ())), preferred_element_type=jnp.float32)


def t_dot(a, b):
    return lax.dot_general(a, b, (((0,), (0,)), ((), ())), preferred_element_type=jnp.float32)


def prep_kernel(tok, cot, tab, order, spread, flag, x_out, g_out, bias_out, lines, rows):
    lines[...] = jnp.zeros_like(lines)
    for source, target in ((tok, x_out), (cot, g_out)):
        for k in range(LINES):
            lines[k, 0:WW, :] = source[k // WH, k % WH]
        flat = lines[...].reshape(LINES * LINE, lines.shape[2])
        target[...] = dot(order[...], flat).astype(jnp.bfloat16)
    rows[...] = jnp.zeros_like(rows)
    key = lax.broadcasted_iota(jnp.int32, (ROWS, ROWS), 1)
    query = lax.broadcasted_iota(jnp.int32, (ROWS, ROWS), 0)
    pad = key % QR >= GROUPS * SW
    apart = (key // (2 * QR)) != (query // (2 * QR))
    drop_two = pad | (apart & (flag[0] == 1))

    def one_head(n, carry):
        base = jnp.broadcast_to(tab[n], (8, TABLE))
        base = pltpu.roll(base, 0, 1, stride=1, stride_axis=0)
        for row, shift in group_list():
            rows[row : row + SW, :] = pltpu.roll(base, TABLE - shift, 1)[:SW, :SPAN]
        wide = rows[...]
        high = wide.astype(jnp.bfloat16)
        rest = wide - high.astype(jnp.float32)
        mid = rest.astype(jnp.bfloat16)
        low = (rest - mid.astype(jnp.float32)).astype(jnp.bfloat16)
        part = spread[...]
        bias = dot(high, part) + dot(mid, part) + dot(low, part)
        bias_out[n] = bias
        return carry

    lax.fori_loop(0, 2 * H, one_head, 0)

    def mask_head(n, carry):
        bias_out[n] = jnp.where(pad, FAR, bias_out[n])
        bias_out[n + H] = jnp.where(drop_two, FAR, bias_out[n + H])
        return carry

    lax.fori_loop(0, H, mask_head, 0)


def normalise(values):
    centred = values - jnp.mean(values, -1, keepdims=True)
    inverse = lax.rsqrt(jnp.mean(centred * centred, -1, keepdims=True) + EPS)
    return centred * inverse, inverse


def half_mask(which):
    lane = lax.broadcasted_iota(jnp.int32, (ROWS, 2 * HD), 1)
    return (lane // HD) == which


def forward_kernel(x_ref, gain, w_in, w_proj, bias, y_out, qkv, probs, ctx):
    normed, _ = normalise(x_ref[...].astype(jnp.float32))
    qkv[...] = dot((normed * gain[...]).astype(jnp.bfloat16), w_in[...]).astype(jnp.bfloat16)
    first_half = half_mask(0)
    for pair in range(H // 2):
        lo, hi = pair * 2 * HD, (pair + 1) * 2 * HD
        query = qkv[:, lo:hi] * jnp.bfloat16(SCALE)
        keys = qkv[:, H * HD + lo : H * HD + hi]
        values = qkv[:, 2 * H * HD + lo : 2 * H * HD + hi]
        found = []
        for side in range(2):
            keep = first_half if side == 0 else ~first_half
            scores = dot_t(jnp.where(keep, query, 0), keys) + bias[2 * pair + side]
            powers = jnp.exp(scores - jnp.max(scores, -1, keepdims=True))
            weights = (powers / jnp.sum(powers, -1, keepdims=True)).astype(jnp.bfloat16)
            probs[2 * pair + side] = weights
            found.append(dot(weights, values))
        ctx[:, lo:hi] = jnp.where(first_half, found[0], found[1]).astype(jnp.bfloat16)
    y_out[...] = (x_ref[...].astype(jnp.float32) + dot(ctx[...], w_proj[...])).astype(jnp.bfloat16)


def backward_core(g_ref, x_ref, gain, w_in, w_proj, qkv, probs, collect, gain_out, table_out,
                  gctx, gqkv, wide):
    gctx[...] = dot_t(g_ref[...], w_proj[...]).astype(jnp.bfloat16)
    first_half = half_mask(0)
    row_in_group = lax.broadcasted_iota(jnp.int32, (8, SPAN), 0) < SW
    zeros = jnp.zeros((8, TABLE - SPAN), jnp.float32)
    for pair in range(H // 2):
        lo, hi = pair * 2 * HD, (pair + 1) * 2 * HD
        query = qkv[:, lo:hi]
        keys = qkv[:, H * HD + lo : H * HD + hi]
        values = qkv[:, 2 * H * HD + lo : 2 * H * HD + hi]
        part = gctx[:, lo:hi]
        grads = []
        for side in range(2):
            head = 2 * pair + side
            keep = first_half if side == 0 else ~first_half
            weights_bf = probs[head]
            weights = weights_bf.astype(jnp.float32)
            grad_probs = dot_t(jnp.where(keep, part, 0), values)
            grad_scores = weights * (
                grad_probs - jnp.sum(grad_probs * weights, -1, keepdims=True)
            )
            s = grad_scores.astype(jnp.bfloat16)
            rest = (grad_scores - s.astype(jnp.float32)).astype(jnp.bfloat16)
            wide[head] = dot(s, collect[...]) + dot(rest, collect[...])
            grads.append((dot(s, keys), t_dot(s, query), t_dot(weights_bf, part)))
        for which, factor in ((0, SCALE), (1, SCALE), (2, 1.0)):
            both = jnp.where(first_half, grads[0][which], grads[1][which]) * factor
            at = which * H * HD
            gqkv[:, at + lo : at + hi] = both.astype(jnp.bfloat16)

    def fold(head, carry):
        total = jnp.zeros((8, TABLE), jnp.float32)
        for row, shift in group_list():
            rows = jnp.where(row_in_group, wide[head, row : row + 8, :], 0.0)
            total = total + pltpu.roll(jnp.concatenate([rows, zeros], 1), shift, 1)
        line = total[0:1]
        for x in range(1, SW):
            line = line + pltpu.roll(total[x : x + 1], TABLE - x, 1)
        table_out[head] = line
        return carry

    lax.fori_loop(0, H, fold, 0)
    grad_u = dot_t(gqkv[...], w_in[...])
    normed, inverse = normalise(x_ref[...].astype(jnp.float32))
    gain_out[...] = jnp.sum(grad_u * normed, 0, keepdims=True)
    scaled = grad_u * gain[...]
    return g_ref[...].astype(jnp.float32) + inverse * (
        scaled
        - jnp.mean(scaled, -1, keepdims=True)
        - normed * jnp.mean(scaled * normed, -1, keepdims=True)
    )


def backward_kernel(g_ref, x_ref, gain, w_in, w_proj, qkv, probs, collect,
                    gx_out, gain_out, table_out, gctx, gqkv, wide):
    grad = backward_core(g_ref, x_ref, gain, w_in, w_proj, qkv, probs, collect, gain_out,
                         table_out, gctx, gqkv, wide)
    gx_out[...] = grad.astype(jnp.bfloat16)


def last_kernel(g_ref, x_ref, gain, w_in, w_proj, qkv, probs, collect, y_ref, order,
                gx_out, gain_out, table_out, y_out, gctx, gqkv, wide):
    grad = backward_core(g_ref, x_ref, gain, w_in, w_proj, qkv, probs, collect, gain_out,
                         table_out, gctx, gqkv, wide)
    for source, target in ((grad.astype(jnp.bfloat16), gx_out), (y_ref[...], y_out)):
        lines = t_dot(order[...], source).astype(jnp.bfloat16)
        for k in range(LINES):
            target[k // WH, k % WH] = lines[k * LINE : k * LINE + WW]


def exchange_kernel(ahead, src, dst, send, recv, own):
    lat, lon = lax.axis_index("lat"), lax.axis_index("lon")
    lats, lons = lax.axis_size("lat"), lax.axis_size("lon")

    def to(quad, sign):
        y, x = quad // 2, quad % 2
        if ahead:
            dy, dx = 1 - y, 1 - x
        else:
            dy, dx = y, x
        return {
            "lat": lax.rem(lat + lats + sign * dy, lats),
            "lon": lax.rem(lon + lons + sign * dx, lons),
        }

    sign = -1 if ahead else 1
    moving = [quad for quad in range(4) if quad != (3 if ahead else 0)]
    barrier = pltpu.get_barrier_semaphore()
    for quad in moving:
        pl.semaphore_signal(barrier, inc=1, device_id=to(quad, -sign), device_id_type=MESH)
    stay = 3 if ahead else 0
    local = pltpu.make_async_copy(src.at[stay], dst.at[3 - stay], own)
    local.start()
    pl.semaphore_wait(barrier, 3)
    copies = []
    for n, quad in enumerate(moving):
        copies.append(
            pltpu.make_async_remote_copy(
                src_ref=src.at[quad],
                dst_ref=dst.at[3 - quad],
                send_sem=send.at[n],
                recv_sem=recv.at[n],
                device_id=to(quad, sign),
                device_id_type=MESH,
            )
        )
        copies[-1].start()
    local.wait()
    for copy in copies:
        copy.wait()


def exchange(field, ahead, number):
    quads = field.reshape(4, QR, field.shape[-1])
    moved = pl.pallas_call(
        functools.partial(exchange_kernel, ahead),
        out_shape=jax.ShapeDtypeStruct(quads.shape, quads.dtype),
        in_specs=[pl.BlockSpec(memory_space=pltpu.VMEM)],
        out_specs=pl.BlockSpec(memory_space=pltpu.VMEM),
        scratch_shapes=[
            pltpu.SemaphoreType.DMA((3,)),
            pltpu.SemaphoreType.DMA((3,)),
            pltpu.SemaphoreType.DMA,
        ],
        compiler_params=pltpu.CompilerParams(collective_id=number, has_side_effects=True),
    )(quads)
    return moved.reshape(field.shape)


def call(kernel, out, scratch, args, smem=(), flops=10**9):
    specs = [
        pl.BlockSpec(memory_space=pltpu.SMEM if n in smem else pltpu.VMEM)
        for n in range(len(args))
    ]
    return pl.pallas_call(
        kernel,
        out_shape=[jax.ShapeDtypeStruct(shape, dtype) for shape, dtype in out],
        in_specs=specs,
        out_specs=[pl.BlockSpec(memory_space=pltpu.VMEM) for _ in out],
        scratch_shapes=[pltpu.VMEM(shape, dtype) for shape, dtype in scratch],
        compiler_params=pltpu.CompilerParams(vmem_limit_bytes=VMEM_LIMIT),
        cost_estimate=pl.CostEstimate(flops=flops, bytes_accessed=8 * 2**20, transcendentals=0),
    )(*args)


def shift_quads(field, ahead):
    lats, lons = lax.axis_size("lat"), lax.axis_size("lon")
    quads = field.reshape(4, QR, field.shape[-1])
    sign = -1 if ahead else 1
    arrived = []
    for slot in range(4):
        quad = 3 - slot
        y, x = quad // 2, quad % 2
        dy, dx = (1 - y, 1 - x) if ahead else (y, x)
        if dy == 0 and dx == 0:
            arrived.append(quads[quad])
            continue
        pairs = []
        for lat in range(lats):
            for lon in range(lons):
                target = ((lat + sign * dy) % lats) * lons + (lon + sign * dx) % lons
                pairs.append((lat * lons + lon, target))
        arrived.append(lax.ppermute(quads[quad], ("lat", "lon"), pairs))
    return jnp.concatenate(arrived, 0)


def peers_of(axis):
    me, size = lax.axis_index(axis), lax.axis_size(axis)
    ahead = [(d, lax.rem(me + d, size)) for d in range(1, size)]
    behind = [(d, lax.rem(me + size - d, size)) for d in range(1, size)]
    return me, ahead, behind


def greet(axes):
    barrier = pltpu.get_barrier_semaphore()
    count = 0
    for axis in axes:
        for _, peer in peers_of(axis)[1]:
            pl.semaphore_signal(barrier, inc=1, device_id={axis: peer}, device_id_type=MESH)
            count += 1
    pl.semaphore_wait(barrier, count)


def gather_kernel(w_in, w_proj, full_in, full_proj, send_z, recv_z, send_p, recv_p, send_c,
                  recv_c, own):
    dp, dp_ahead, _ = peers_of("dp")
    lat, lat_ahead, _ = peers_of("lat")
    lon, lon_ahead, lon_behind = peers_of("lon")
    lons = lax.axis_size("lon")
    arrays = ((w_in, full_in), (w_proj, full_proj))
    mine = lat * lons + lon
    greet(("dp", "lat", "lon"))
    sent = []

    def put(src, dst, send, recv, device):
        copy = pltpu.make_async_remote_copy(
            src_ref=src, dst_ref=dst, send_sem=send, recv_sem=recv, device_id=device,
            device_id_type=MESH,
        )
        copy.start()
        sent.append(copy)
        return copy

    along = {}
    for d, peer in lon_ahead:
        for n, (part, full) in enumerate(arrays):
            along[d, n] = put(part.at[0, dp], full.at[mine, dp], send_z.at[n, d], recv_z.at[n, d],
                              {"lon": peer})
    local = []
    across = []
    for n, (part, full) in enumerate(arrays):
        local.append(pltpu.make_async_copy(part.at[0], full.at[mine], own.at[n]))
        local[-1].start()
        for f, peer in lat_ahead:
            across.append(put(part.at[0], full.at[mine], send_c.at[n, 0, f], recv_c.at[n, 0, f],
                              {"lat": peer}))
    plane = {}
    for d, source in lon_behind:
        shard = lat * lons + source
        for n, (_, full) in enumerate(arrays):
            along[d, n].wait_recv()
            for e, peer in dp_ahead:
                plane[d, n, e] = put(full.at[shard, dp], full.at[shard, dp], send_p.at[n, d, e],
                                     recv_p.at[n, d, e], {"dp": peer})
    for d, source in lon_behind:
        shard = lat * lons + source
        for n, (_, full) in enumerate(arrays):
            for e, _ in dp_ahead:
                plane[d, n, e].wait_recv()
            for f, peer in lat_ahead:
                across.append(put(full.at[shard], full.at[shard], send_c.at[n, d, f],
                                  recv_c.at[n, d, f], {"lat": peer}))
    for copy in local:
        copy.wait()
    for copy in across:
        copy.wait_recv()
    for copy in sent:
        copy.wait_send()


def fetch_first(w_qkv, w_out):
    dps, lats, lons = (lax.axis_size(axis) for axis in ("dp", "lat", "lon"))
    shards = lats * lons
    if w_qkv.shape[1] % (16 * dps) or w_out.shape[1] % (16 * dps):
        return fetch_block(w_qkv, w_out, 0)
    parts = [w.reshape(2, dps, w.shape[1] // dps, w.shape[2]) for w in (w_qkv, w_out)]
    dma = pltpu.SemaphoreType.DMA
    full = pl.pallas_call(
        gather_kernel,
        out_shape=[
            jax.ShapeDtypeStruct((shards,) + part.shape[1:], part.dtype) for part in parts
        ],
        in_specs=[pl.BlockSpec(memory_space=pltpu.VMEM)] * 2,
        out_specs=[pl.BlockSpec(memory_space=pltpu.VMEM)] * 2,
        scratch_shapes=[
            dma((2, lons)), dma((2, lons)), dma((2, lons, dps)), dma((2, lons, dps)),
            dma((2, lons, lats)), dma((2, lons, lats)), dma((2,)),
        ],
        compiler_params=pltpu.CompilerParams(
            collective_id=5, has_side_effects=True, vmem_limit_bytes=VMEM_LIMIT
        ),
    )(*parts)
    return tuple(array.reshape(-1, array.shape[-1]) for array in full)


def reduce_kernel(data, total, from_lat, lat_sum, from_dp, from_lon, lat_all, send, recv):
    dp, dp_ahead, dp_behind = peers_of("dp")
    lat, lat_ahead, lat_behind = peers_of("lat")
    lon, lon_ahead, _ = peers_of("lon")
    lons = lax.axis_size("lon")
    greet(("dp", "lat", "lon"))
    sent = []

    def swap(phase, axis, ahead, pick, place):
        copies = []
        for d, peer in ahead:
            copies.append(
                pltpu.make_async_remote_copy(
                    src_ref=pick(peer), dst_ref=place, send_sem=send.at[phase, d],
                    recv_sem=recv.at[phase, d], device_id={axis: peer}, device_id_type=MESH,
                )
            )
            copies[-1].start()
        for copy in copies:
            copy.wait_recv()
        sent.extend(copies)

    swap(0, "lat", lat_ahead, lambda peer: data.at[peer], from_lat.at[lat])
    value = data[lat]
    for _, peer in lat_behind:
        value = value + from_lat[peer]
    lat_sum[...] = value
    swap(1, "dp", dp_ahead, lambda peer: lat_sum.at[peer], from_dp.at[dp])
    value = lat_sum[dp]
    for _, peer in dp_behind:
        value = value + from_dp[peer]
    from_lon[lon] = value
    swap(2, "lon", lon_ahead, lambda peer: from_lon.at[lon], from_lon.at[lon])
    value = from_lon[0]
    for n in range(1, lons):
        value = value + from_lon[n]
    lat_all[dp] = value
    swap(3, "dp", dp_ahead, lambda peer: lat_all.at[dp], lat_all.at[dp])
    total[lat] = lat_all[...]
    swap(4, "lat", lat_ahead, lambda peer: lat_all, total.at[lat])
    for copy in sent:
        copy.wait_send()


def sum_all(packed):
    dps, lats, lons = (lax.axis_size(axis) for axis in ("dp", "lat", "lon"))
    length = packed.shape[1]
    rows = -(-length // (128 * 8 * dps * lats)) * 8
    padded = jnp.pad(packed[0], (0, rows * 128 * dps * lats - length))
    most = max(dps, lats, lons)
    f32 = jnp.float32
    piece = (rows, 128)
    total = pl.pallas_call(
        reduce_kernel,
        out_shape=jax.ShapeDtypeStruct((lats, dps) + piece, f32),
        in_specs=[pl.BlockSpec(memory_space=pltpu.VMEM)],
        out_specs=pl.BlockSpec(memory_space=pltpu.VMEM),
        scratch_shapes=[
            pltpu.VMEM((lats, dps) + piece, f32),
            pltpu.VMEM((dps,) + piece, f32),
            pltpu.VMEM((dps,) + piece, f32),
            pltpu.VMEM((lons,) + piece, f32),
            pltpu.VMEM((dps,) + piece, f32),
            pltpu.SemaphoreType.DMA((5, most)),
            pltpu.SemaphoreType.DMA((5, most)),
        ],
        compiler_params=pltpu.CompilerParams(collective_id=6, has_side_effects=True),
    )(padded.reshape((lats, dps) + piece))
    return total.reshape(1, -1)[:, :length]


def fetch_block(w_qkv, w_out, index):
    return (
        lax.all_gather(w_qkv[index], ("lat", "lon"), axis=0, tiled=True),
        lax.all_gather(w_out[index], ("lat", "lon"), axis=0, tiled=True),
    )


def on_device(tokens, cotangent, w_qkv, w_out, gains, tables):
    features = tokens.shape[-1]
    bf, f32 = jnp.bfloat16, jnp.float32
    inner = H * HD
    order = jnp.asarray(order_matrix(), bf)
    spread = jnp.asarray(spread_matrix(), bf)
    collect = jnp.asarray(spread_matrix().T.copy(), bf)
    in_one, proj_one = fetch_first(w_qkv, w_out)
    in_two, proj_two = fetch_block(w_qkv, w_out, 1)
    polar = lax.axis_index("lat") == lax.axis_size("lat") - 1
    flag = jnp.where(polar, 1, 0).astype(jnp.int32).reshape(1)
    lines = jnp.pad(tables.reshape(2 * H, 1, RELS)[:, :, ::-1], ((0, 0), (0, 0), (0, TABLE - RELS)))
    field = ((ROWS, features), bf)
    x_one, g_out, bias = call(
        prep_kernel,
        [field, field, ((2 * H, ROWS, ROWS), f32)],
        [((LINES, LINE, features), bf), ((ROWS, SPAN), f32)],
        (tokens[0], cotangent[0], lines, order, spread, flag),
        smem=(5,),
        flops=8 * 10**9,
    )
    saved = [((ROWS, 3 * inner), bf), ((H, ROWS, ROWS), bf)]
    wide = [((ROWS, inner), bf)]
    g_two = shift_quads(g_out, True)
    gain_one, gain_two = gains[0:1], gains[1:2]
    first, qkv_one, probs_one = call(
        forward_kernel, [field] + saved, wide, (x_one, gain_one, in_one, proj_one, bias[:H])
    )
    x_two = exchange(first, True, 1)
    second, qkv_two, probs_two = call(
        forward_kernel, [field] + saved, wide, (x_two, gain_two, in_two, proj_two, bias[H:])
    )
    y_back = shift_quads(second, False)
    back = [((ROWS, inner), bf), ((ROWS, 3 * inner), bf), ((H, ROWS, SPAN), f32)]
    terms = [((1, features), f32), ((H, 1, TABLE), f32)]
    gx_two, gterm_two, tterm_two = call(
        backward_kernel,
        [field] + terms,
        back,
        (g_two, x_two, gain_two, in_two, proj_two, qkv_two, probs_two, collect),
    )
    g_one = exchange(gx_two, False, 3)
    window = (tokens.shape[1:], bf)
    grad_tokens, gterm_one, tterm_one, outputs = call(
        last_kernel,
        [window] + terms + [window],
        back,
        (g_one, x_one, gain_one, in_one, proj_one, qkv_one, probs_one, collect, y_back, order),
    )
    packed = jnp.concatenate(
        [gterm_one, gterm_two, tterm_one.reshape(1, -1), tterm_two.reshape(1, -1)], 1
    )
    packed = sum_all(packed)
    total = math.prod(tokens.shape[:4]) * math.prod(
        lax.axis_size(axis) for axis in ("dp", "lat", "lon")
    )
    packed = packed * (1.0 / math.sqrt(total))
    grad_gains = packed[:, : 2 * features].reshape(2, features)
    folded = packed[:, 2 * features :].reshape(2, H, TABLE)
    grad_tables = folded[:, :, :RELS][:, :, ::-1]
    return (outputs[None], grad_tokens[None], grad_gains, grad_tables)


def solution(mesh):
    return jax.shard_map(
        on_device,
        mesh=mesh,
        in_specs=(
            P("dp", None, "lat", "lon", None),
            P("dp", None, "lat", "lon", None),
            P(None, ("lat", "lon"), None),
            P(None, ("lat", "lon"), None),
            P(),
            P(),
        ),
        out_specs=(P("dp", None, "lat", "lon", None), P("dp", None, "lat", "lon", None), P(), P()),
        check_vma=False,
    )
```

```python
import functools
import math

import jax
import jax.numpy as jnp
import numpy as np
from jax import lax
from jax.experimental import pallas as pl
from jax.experimental.pallas import tpu as pltpu
from jax.sharding import PartitionSpec as P

MESH = pl.DeviceIdType.MESH
HD = 64
H = 8
Z = 3
WH = 6
WW = 12
SH = 3
SW = 6
EPS = 1e-05
RELS = (2 * Z - 1) * (2 * WH - 1) * (2 * WW - 1)
STEP_Z = (2 * WH - 1) * (2 * WW - 1)
STEP_Y = 2 * WW - 1
CENTRE = (Z - 1) * STEP_Z + (WH - 1) * STEP_Y + WW - 1
QR = 64
ROWS = 4 * QR
SPAN = 640
TABLE = 1280
GROUPS = Z * SH
LINES = Z * WH
LINE = 16
SCALE = HD ** (-0.5)
FAR = -1e30
VMEM_LIMIT = 58 * 1024 * 1024


def token_places():
    places = []
    for row in range(ROWS):
        quad, inner = divmod(row, QR)
        if inner >= GROUPS * SW:
            places.append(None)
            continue
        group, x = divmod(inner, SW)
        z, y = divmod(group, SH)
        places.append((z, y + SH * (quad // 2), x + SW * (quad % 2)))
    return places


def order_matrix():
    order = np.zeros((ROWS, LINES * LINE), np.float32)
    for row, place in enumerate(token_places()):
        if place is not None:
            z, y, x = place
            order[row, (z * WH + y) * LINE + x] = 1
    return order


def spread_matrix():
    spread = np.zeros((SPAN, ROWS), np.float32)
    for row, place in enumerate(token_places()):
        if place is not None:
            z, y, x = place
            spread[z * STEP_Z + y * STEP_Y + x, row] = 1
    return spread


def group_list():
    groups = []
    for quad in range(4):
        for group in range(GROUPS):
            z, y = divmod(group, SH)
            start = z * STEP_Z + (y + SH * (quad // 2)) * STEP_Y + SW * (quad % 2)
            groups.append((quad * QR + group * SW, CENTRE - start))
    return groups


def dot(a, b):
    return jnp.dot(a, b, preferred_element_type=jnp.float32)


def dot_t(a, b):
    return lax.dot_general(a, b, (((1,), (1,)), ((), ())), preferred_element_type=jnp.float32)


def t_dot(a, b):
    return lax.dot_general(a, b, (((0,), (0,)), ((), ())), preferred_element_type=jnp.float32)


STAGES = (5, 11, 2 * H)


def prep_stage(stage, tok, cot, tab, order, spread, x_out, g_out, bias_one, bias_two, lines, rows):
    if stage == 0:
        lines[...] = jnp.zeros_like(lines)
        for source, target in ((tok, x_out), (cot, g_out)):
            for k in range(LINES):
                lines[k, 0:WW, :] = source[k // WH, k % WH]
            flat = lines[...].reshape(LINES * LINE, lines.shape[2])
            target[...] = dot(order[...], flat).astype(jnp.bfloat16)
        rows[...] = jnp.zeros_like(rows)
    key = lax.broadcasted_iota(jnp.int32, (ROWS, ROWS), 1)
    query = lax.broadcasted_iota(jnp.int32, (ROWS, ROWS), 0)
    pad = key % QR >= GROUPS * SW
    polar = jnp.where(lax.axis_index("lat") == lax.axis_size("lat") - 1, 1, 0)
    apart = jnp.where((key // (2 * QR)) != (query // (2 * QR)), polar, 0)
    drops = (pad, pad | (apart == 1))

    def one_head(block, target, n, carry):
        base = jnp.broadcast_to(tab[block * H + n], (8, TABLE))
        base = pltpu.roll(base, 0, 1, stride=1, stride_axis=0)
        for row, shift in group_list():
            rows[row : row + SW, :] = pltpu.roll(base, TABLE - shift, 1)[:SW, :SPAN]
        wide = rows[...]
        high = wide.astype(jnp.bfloat16)
        rest = wide - high.astype(jnp.float32)
        mid = rest.astype(jnp.bfloat16)
        low = (rest - mid.astype(jnp.float32)).astype(jnp.bfloat16)
        part = spread[...]
        bias = dot(high, part) + dot(mid, part) + dot(low, part)
        target[n] = jnp.where(drops[block], FAR, bias)
        return carry

    first = 0 if stage == 0 else STAGES[stage - 1]
    last = STAGES[stage]
    for block, target in ((0, bias_one), (1, bias_two)):
        low, high = max(first - block * H, 0), min(last - block * H, H)
        if low < high:
            lax.fori_loop(low, high, functools.partial(one_head, block, target), 0)


def prep_kernel(*refs):
    for stage in range(len(STAGES)):
        prep_stage(stage, *refs)


def normalise(values):
    centred = values - jnp.mean(values, -1, keepdims=True)
    inverse = lax.rsqrt(jnp.mean(centred * centred, -1, keepdims=True) + EPS)
    return centred * inverse, inverse


def half_mask(which):
    lane = lax.broadcasted_iota(jnp.int32, (ROWS, 2 * HD), 1)
    return (lane // HD) == which


def forward_kernel(x_ref, gain, w_in, w_proj, bias, y_out, qkv, probs, ctx):
    normed, _ = normalise(x_ref[...].astype(jnp.float32))
    qkv[...] = dot((normed * gain[...]).astype(jnp.bfloat16), w_in[...]).astype(jnp.bfloat16)
    first_half = half_mask(0)
    for pair in range(H // 2):
        lo, hi = pair * 2 * HD, (pair + 1) * 2 * HD
        query = qkv[:, lo:hi] * jnp.bfloat16(SCALE)
        keys = qkv[:, H * HD + lo : H * HD + hi]
        values = qkv[:, 2 * H * HD + lo : 2 * H * HD + hi]
        found = []
        for side in range(2):
            keep = first_half if side == 0 else ~first_half
            scores = dot_t(jnp.where(keep, query, 0), keys) + bias[2 * pair + side]
            powers = jnp.exp(scores - jnp.max(scores, -1, keepdims=True))
            weights = (powers / jnp.sum(powers, -1, keepdims=True)).astype(jnp.bfloat16)
            probs[2 * pair + side] = weights
            found.append(dot(weights, values))
        ctx[:, lo:hi] = jnp.where(first_half, found[0], found[1]).astype(jnp.bfloat16)
    y_out[...] = (x_ref[...].astype(jnp.float32) + dot(ctx[...], w_proj[...])).astype(jnp.bfloat16)


def backward_core(g_ref, x_ref, gain, w_in, w_proj, qkv, probs, collect, gain_out, table_out,
                  gctx, gqkv, wide):
    gctx[...] = dot_t(g_ref[...], w_proj[...]).astype(jnp.bfloat16)
    first_half = half_mask(0)
    row_in_group = lax.broadcasted_iota(jnp.int32, (8, SPAN), 0) < SW
    zeros = jnp.zeros((8, TABLE - SPAN), jnp.float32)
    for pair in range(H // 2):
        lo, hi = pair * 2 * HD, (pair + 1) * 2 * HD
        query = qkv[:, lo:hi]
        keys = qkv[:, H * HD + lo : H * HD + hi]
        values = qkv[:, 2 * H * HD + lo : 2 * H * HD + hi]
        part = gctx[:, lo:hi]
        grads = []
        for side in range(2):
            head = 2 * pair + side
            keep = first_half if side == 0 else ~first_half
            weights_bf = probs[head]
            weights = weights_bf.astype(jnp.float32)
            grad_probs = dot_t(jnp.where(keep, part, 0), values)
            grad_scores = weights * (
                grad_probs - jnp.sum(grad_probs * weights, -1, keepdims=True)
            )
            s = grad_scores.astype(jnp.bfloat16)
            rest = (grad_scores - s.astype(jnp.float32)).astype(jnp.bfloat16)
            wide[head] = dot(s, collect[...]) + dot(rest, collect[...])
            grads.append((dot(s, keys), t_dot(s, query), t_dot(weights_bf, part)))
        for which, factor in ((0, SCALE), (1, SCALE), (2, 1.0)):
            both = jnp.where(first_half, grads[0][which], grads[1][which]) * factor
            at = which * H * HD
            gqkv[:, at + lo : at + hi] = both.astype(jnp.bfloat16)

    def fold(head, carry):
        total = jnp.zeros((8, TABLE), jnp.float32)
        for row, shift in group_list():
            rows = jnp.where(row_in_group, wide[head, row : row + 8, :], 0.0)
            total = total + pltpu.roll(jnp.concatenate([rows, zeros], 1), shift, 1)
        line = total[0:1]
        for x in range(1, SW):
            line = line + pltpu.roll(total[x : x + 1], TABLE - x, 1)
        table_out[head] = line
        return carry

    lax.fori_loop(0, H, fold, 0)
    grad_u = dot_t(gqkv[...], w_in[...])
    normed, inverse = normalise(x_ref[...].astype(jnp.float32))
    gain_out[...] = jnp.sum(grad_u * normed, 0, keepdims=True)
    scaled = grad_u * gain[...]
    return g_ref[...].astype(jnp.float32) + inverse * (
        scaled
        - jnp.mean(scaled, -1, keepdims=True)
        - normed * jnp.mean(scaled * normed, -1, keepdims=True)
    )


def backward_kernel(g_ref, x_ref, gain, w_in, w_proj, qkv, probs, collect,
                    gx_out, gain_out, table_out, gctx, gqkv, wide):
    grad = backward_core(g_ref, x_ref, gain, w_in, w_proj, qkv, probs, collect, gain_out,
                         table_out, gctx, gqkv, wide)
    gx_out[...] = grad.astype(jnp.bfloat16)


def last_kernel(g_ref, x_ref, gain, w_in, w_proj, qkv, probs, collect, y_ref, order,
                gx_out, gain_out, table_out, y_out, gctx, gqkv, wide):
    grad = backward_core(g_ref, x_ref, gain, w_in, w_proj, qkv, probs, collect, gain_out,
                         table_out, gctx, gqkv, wide)
    for source, target in ((grad.astype(jnp.bfloat16), gx_out), (y_ref[...], y_out)):
        lines = t_dot(order[...], source).astype(jnp.bfloat16)
        for k in range(LINES):
            target[k // WH, k % WH] = lines[k * LINE : k * LINE + WW]


def exchange_kernel(ahead, src, dst, send, recv, own):
    lat, lon = lax.axis_index("lat"), lax.axis_index("lon")
    lats, lons = lax.axis_size("lat"), lax.axis_size("lon")

    def to(quad, sign):
        y, x = quad // 2, quad % 2
        if ahead:
            dy, dx = 1 - y, 1 - x
        else:
            dy, dx = y, x
        return {
            "lat": lax.rem(lat + lats + sign * dy, lats),
            "lon": lax.rem(lon + lons + sign * dx, lons),
        }

    sign = -1 if ahead else 1
    moving = [quad for quad in range(4) if quad != (3 if ahead else 0)]
    barrier = pltpu.get_barrier_semaphore()
    for quad in moving:
        pl.semaphore_signal(barrier, inc=1, device_id=to(quad, -sign), device_id_type=MESH)
    stay = 3 if ahead else 0
    local = pltpu.make_async_copy(src.at[stay], dst.at[3 - stay], own)
    local.start()
    pl.semaphore_wait(barrier, 3)
    copies = []
    for n, quad in enumerate(moving):
        copies.append(
            pltpu.make_async_remote_copy(
                src_ref=src.at[quad],
                dst_ref=dst.at[3 - quad],
                send_sem=send.at[n],
                recv_sem=recv.at[n],
                device_id=to(quad, sign),
                device_id_type=MESH,
            )
        )
        copies[-1].start()
    local.wait()
    for copy in copies:
        copy.wait()


def exchange(field, ahead, number):
    quads = field.reshape(4, QR, field.shape[-1])
    moved = pl.pallas_call(
        functools.partial(exchange_kernel, ahead),
        out_shape=jax.ShapeDtypeStruct(quads.shape, quads.dtype),
        in_specs=[pl.BlockSpec(memory_space=pltpu.VMEM)],
        out_specs=pl.BlockSpec(memory_space=pltpu.VMEM),
        scratch_shapes=[
            pltpu.SemaphoreType.DMA((3,)),
            pltpu.SemaphoreType.DMA((3,)),
            pltpu.SemaphoreType.DMA,
        ],
        compiler_params=pltpu.CompilerParams(collective_id=number, has_side_effects=True),
    )(quads)
    return moved.reshape(field.shape)


def call(kernel, out, scratch, args, smem=(), flops=10**9):
    specs = [
        pl.BlockSpec(memory_space=pltpu.SMEM if n in smem else pltpu.VMEM)
        for n in range(len(args))
    ]
    return pl.pallas_call(
        kernel,
        out_shape=[jax.ShapeDtypeStruct(shape, dtype) for shape, dtype in out],
        in_specs=specs,
        out_specs=[pl.BlockSpec(memory_space=pltpu.VMEM) for _ in out],
        scratch_shapes=[pltpu.VMEM(shape, dtype) for shape, dtype in scratch],
        compiler_params=pltpu.CompilerParams(vmem_limit_bytes=VMEM_LIMIT),
        cost_estimate=pl.CostEstimate(flops=flops, bytes_accessed=8 * 2**20, transcendentals=0),
    )(*args)


def shift_quads(field, ahead):
    lats, lons = lax.axis_size("lat"), lax.axis_size("lon")
    quads = field.reshape(4, QR, field.shape[-1])
    sign = -1 if ahead else 1
    arrived = []
    for slot in range(4):
        quad = 3 - slot
        y, x = quad // 2, quad % 2
        dy, dx = (1 - y, 1 - x) if ahead else (y, x)
        if dy == 0 and dx == 0:
            arrived.append(quads[quad])
            continue
        pairs = []
        for lat in range(lats):
            for lon in range(lons):
                target = ((lat + sign * dy) % lats) * lons + (lon + sign * dx) % lons
                pairs.append((lat * lons + lon, target))
        arrived.append(lax.ppermute(quads[quad], ("lat", "lon"), pairs))
    return jnp.concatenate(arrived, 0)


def peers_of(axis):
    me, size = lax.axis_index(axis), lax.axis_size(axis)
    ahead = [(d, lax.rem(me + d, size)) for d in range(1, size)]
    behind = [(d, lax.rem(me + size - d, size)) for d in range(1, size)]
    return me, ahead, behind


def greet(axes):
    barrier = pltpu.get_barrier_semaphore()
    count = 0
    for axis in axes:
        for _, peer in peers_of(axis)[1]:
            pl.semaphore_signal(barrier, inc=1, device_id={axis: peer}, device_id_type=MESH)
            count += 1
    pl.semaphore_wait(barrier, count)


def gather_kernel(w_in, w_proj, tok, cot, tab, order, spread, full_in, full_proj, x_out, g_out,
                  bias_one, bias_two, lines, rows, send_z, recv_z, send_p, recv_p, send_c,
                  recv_c, own):
    prep = functools.partial(prep_stage, tok=tok, cot=cot, tab=tab, order=order, spread=spread,
                             x_out=x_out, g_out=g_out, bias_one=bias_one, bias_two=bias_two,
                             lines=lines, rows=rows)
    dp, dp_ahead, _ = peers_of("dp")
    lat, lat_ahead, _ = peers_of("lat")
    lon, lon_ahead, lon_behind = peers_of("lon")
    lons = lax.axis_size("lon")
    arrays = ((w_in, full_in), (w_proj, full_proj))
    mine = lat * lons + lon
    greet(("dp", "lat", "lon"))
    sent = []

    def put(src, dst, send, recv, device):
        copy = pltpu.make_async_remote_copy(
            src_ref=src, dst_ref=dst, send_sem=send, recv_sem=recv, device_id=device,
            device_id_type=MESH,
        )
        copy.start()
        sent.append(copy)
        return copy

    along = {}
    for d, peer in lon_ahead:
        for n, (part, full) in enumerate(arrays):
            along[d, n] = put(part.at[0, dp], full.at[mine, dp], send_z.at[n, d], recv_z.at[n, d],
                              {"lon": peer})
    local = []
    across = []
    for n, (part, full) in enumerate(arrays):
        local.append(pltpu.make_async_copy(part.at[0], full.at[mine], own.at[n]))
        local[-1].start()
        for f, peer in lat_ahead:
            across.append(put(part.at[0], full.at[mine], send_c.at[n, 0, f], recv_c.at[n, 0, f],
                              {"lat": peer}))
    prep(0)
    plane = {}
    for d, source in lon_behind:
        shard = lat * lons + source
        for n, (_, full) in enumerate(arrays):
            along[d, n].wait_recv()
            for e, peer in dp_ahead:
                plane[d, n, e] = put(full.at[shard, dp], full.at[shard, dp], send_p.at[n, d, e],
                                     recv_p.at[n, d, e], {"dp": peer})
    prep(1)
    for d, source in lon_behind:
        shard = lat * lons + source
        for n, (_, full) in enumerate(arrays):
            for e, _ in dp_ahead:
                plane[d, n, e].wait_recv()
            for f, peer in lat_ahead:
                across.append(put(full.at[shard], full.at[shard], send_c.at[n, d, f],
                                  recv_c.at[n, d, f], {"lat": peer}))
    prep(2)
    for copy in local:
        copy.wait()
    for copy in across:
        copy.wait_recv()
    for copy in sent:
        copy.wait_send()


def fetch_first(w_qkv, w_out, prep_args, prep_out, prep_scratch):
    dps, lats, lons = (lax.axis_size(axis) for axis in ("dp", "lat", "lon"))
    shards = lats * lons
    if w_qkv.shape[1] % (16 * dps) or w_out.shape[1] % (16 * dps):
        full = fetch_block(w_qkv, w_out, 0)
        return full, call(prep_kernel, prep_out, prep_scratch, prep_args, flops=8 * 10**9)
    parts = [w.reshape(2, dps, w.shape[1] // dps, w.shape[2]) for w in (w_qkv, w_out)]
    dma = pltpu.SemaphoreType.DMA
    shapes = [((shards,) + part.shape[1:], part.dtype) for part in parts] + prep_out
    vmem = pl.BlockSpec(memory_space=pltpu.VMEM)
    found = pl.pallas_call(
        gather_kernel,
        out_shape=[jax.ShapeDtypeStruct(shape, dtype) for shape, dtype in shapes],
        in_specs=[vmem] * (2 + len(prep_args)),
        out_specs=[vmem] * len(shapes),
        scratch_shapes=[pltpu.VMEM(shape, dtype) for shape, dtype in prep_scratch]
        + [
            dma((2, lons)), dma((2, lons)), dma((2, lons, dps)), dma((2, lons, dps)),
            dma((2, lons, lats)), dma((2, lons, lats)), dma((2,)),
        ],
        compiler_params=pltpu.CompilerParams(
            collective_id=5, has_side_effects=True, vmem_limit_bytes=VMEM_LIMIT
        ),
    )(*parts, *prep_args)
    return tuple(array.reshape(-1, array.shape[-1]) for array in found[:2]), found[2:]


def plane_peers():
    dps, lats = lax.axis_size("dp"), lax.axis_size("lat")
    dp, lat = lax.axis_index("dp"), lax.axis_index("lat")
    ahead, behind = [], []
    for far in range(1, dps * lats):
        a, b = far // dps, far % dps
        ahead.append((far, lax.rem(lat + a, lats), lax.rem(dp + b, dps)))
        behind.append((far, lax.rem(lat + lats - a, lats), lax.rem(dp + dps - b, dps)))
    return ahead, behind


def reduce_kernel(data, total, from_plane, from_lon, send, recv, send_z, recv_z):
    dp, lat = lax.axis_index("dp"), lax.axis_index("lat")
    ahead, behind = plane_peers()
    lon, lon_ahead, _ = peers_of("lon")
    lons = lax.axis_size("lon")
    barrier = pltpu.get_barrier_semaphore()
    for _, a, b in ahead:
        pl.semaphore_signal(
            barrier, inc=1, device_id={"lat": a, "dp": b}, device_id_type=MESH
        )
    for _, peer in lon_ahead:
        pl.semaphore_signal(barrier, inc=1, device_id={"lon": peer}, device_id_type=MESH)
    pl.semaphore_wait(barrier, len(ahead) + len(lon_ahead))
    sent = []

    def put(src, dst, send_sem, recv_sem, device):
        copy = pltpu.make_async_remote_copy(
            src_ref=src, dst_ref=dst, send_sem=send_sem, recv_sem=recv_sem, device_id=device,
            device_id_type=MESH,
        )
        copy.start()
        sent.append(copy)
        return copy

    first = [
        put(data.at[a, b], from_plane.at[lat, dp], send.at[0, d], recv.at[0, d],
            {"lat": a, "dp": b})
        for d, a, b in ahead
    ]
    value = data[lat, dp]
    for copy in first:
        copy.wait_recv()
    for _, a, b in behind:
        value = value + from_plane[a, b]
    from_lon[lon] = value
    second = [
        put(from_lon.at[lon], from_lon.at[lon], send_z.at[d], recv_z.at[d], {"lon": peer})
        for d, peer in lon_ahead
    ]
    for copy in second:
        copy.wait_recv()
    value = from_lon[0]
    for n in range(1, lons):
        value = value + from_lon[n]
    total[lat, dp] = value
    third = [
        put(total.at[lat, dp], total.at[lat, dp], send.at[1, d], recv.at[1, d],
            {"lat": a, "dp": b})
        for d, a, b in ahead
    ]
    for copy in third:
        copy.wait_recv()
    for copy in sent:
        copy.wait_send()


def sum_all(packed):
    dps, lats, lons = (lax.axis_size(axis) for axis in ("dp", "lat", "lon"))
    length = packed.shape[1]
    rows = -(-length // (128 * 8 * dps * lats)) * 8
    padded = jnp.pad(packed[0], (0, rows * 128 * dps * lats - length))
    f32 = jnp.float32
    piece = (rows, 128)
    total = pl.pallas_call(
        reduce_kernel,
        out_shape=jax.ShapeDtypeStruct((lats, dps) + piece, f32),
        in_specs=[pl.BlockSpec(memory_space=pltpu.VMEM)],
        out_specs=pl.BlockSpec(memory_space=pltpu.VMEM),
        scratch_shapes=[
            pltpu.VMEM((lats, dps) + piece, f32),
            pltpu.VMEM((lons,) + piece, f32),
            pltpu.SemaphoreType.DMA((2, dps * lats)),
            pltpu.SemaphoreType.DMA((2, dps * lats)),
            pltpu.SemaphoreType.DMA((lons,)),
            pltpu.SemaphoreType.DMA((lons,)),
        ],
        compiler_params=pltpu.CompilerParams(collective_id=6, has_side_effects=True),
    )(padded.reshape((lats, dps) + piece))
    return total.reshape(1, -1)[:, :length]


def fetch_block(w_qkv, w_out, index):
    return (
        lax.all_gather(w_qkv[index], ("lat", "lon"), axis=0, tiled=True),
        lax.all_gather(w_out[index], ("lat", "lon"), axis=0, tiled=True),
    )


def on_device(tokens, cotangent, w_qkv, w_out, gains, tables):
    features = tokens.shape[-1]
    bf, f32 = jnp.bfloat16, jnp.float32
    inner = H * HD
    order = jnp.asarray(order_matrix(), bf)
    spread = jnp.asarray(spread_matrix(), bf)
    collect = jnp.asarray(spread_matrix().T.copy(), bf)
    in_two, proj_two = fetch_block(w_qkv, w_out, 1)
    lines = jnp.pad(tables.reshape(2 * H, 1, RELS)[:, :, ::-1], ((0, 0), (0, 0), (0, TABLE - RELS)))
    field = ((ROWS, features), bf)
    bias = ((H, ROWS, ROWS), f32)
    (in_one, proj_one), (x_one, g_out, bias_one, bias_two) = fetch_first(
        w_qkv,
        w_out,
        (tokens[0], cotangent[0], lines, order, spread),
        [field, field, bias, bias],
        [((LINES, LINE, features), bf), ((ROWS, SPAN), f32)],
    )
    saved = [((ROWS, 3 * inner), bf), ((H, ROWS, ROWS), bf)]
    wide = [((ROWS, inner), bf)]
    g_two = shift_quads(g_out, True)
    gain_one, gain_two = gains[0:1], gains[1:2]
    first, qkv_one, probs_one = call(
        forward_kernel, [field] + saved, wide, (x_one, gain_one, in_one, proj_one, bias_one)
    )
    x_two = exchange(first, True, 1)
    second, qkv_two, probs_two = call(
        forward_kernel, [field] + saved, wide, (x_two, gain_two, in_two, proj_two, bias_two)
    )
    y_back = shift_quads(second, False)
    back = [((ROWS, inner), bf), ((ROWS, 3 * inner), bf), ((H, ROWS, SPAN), f32)]
    terms = [((1, features), f32), ((H, 1, TABLE), f32)]
    gx_two, gterm_two, tterm_two = call(
        backward_kernel,
        [field] + terms,
        back,
        (g_two, x_two, gain_two, in_two, proj_two, qkv_two, probs_two, collect),
    )
    g_one = exchange(gx_two, False, 3)
    window = (tokens.shape[1:], bf)
    grad_tokens, gterm_one, tterm_one, outputs = call(
        last_kernel,
        [window] + terms + [window],
        back,
        (g_one, x_one, gain_one, in_one, proj_one, qkv_one, probs_one, collect, y_back, order),
    )
    packed = jnp.concatenate(
        [gterm_one, gterm_two, tterm_one.reshape(1, -1), tterm_two.reshape(1, -1)], 1
    )
    packed = sum_all(packed)
    total = math.prod(tokens.shape[:4]) * math.prod(
        lax.axis_size(axis) for axis in ("dp", "lat", "lon")
    )
    packed = packed * (1.0 / math.sqrt(total))
    grad_gains = packed[:, : 2 * features].reshape(2, features)
    folded = packed[:, 2 * features :].reshape(2, H, TABLE)
    grad_tables = folded[:, :, :RELS][:, :, ::-1]
    return (outputs[None], grad_tokens[None], grad_gains, grad_tables)


def solution(mesh):
    return jax.shard_map(
        on_device,
        mesh=mesh,
        in_specs=(
            P("dp", None, "lat", "lon", None),
            P("dp", None, "lat", "lon", None),
            P(None, ("lat", "lon"), None),
            P(None, ("lat", "lon"), None),
            P(),
            P(),
        ),
        out_specs=(P("dp", None, "lat", "lon", None), P("dp", None, "lat", "lon", None), P(), P()),
        check_vma=False,
    )
```

```python
import functools
import math

import jax
import jax.numpy as jnp
import numpy as np
from jax import lax
from jax.experimental import pallas as pl
from jax.experimental.pallas import tpu as pltpu
from jax.sharding import PartitionSpec as P

MESH = pl.DeviceIdType.MESH
HD = 64
H = 8
Z = 3
WH = 6
WW = 12
SH = 3
SW = 6
EPS = 1e-05
RELS = (2 * Z - 1) * (2 * WH - 1) * (2 * WW - 1)
STEP_Z = (2 * WH - 1) * (2 * WW - 1)
STEP_Y = 2 * WW - 1
CENTRE = (Z - 1) * STEP_Z + (WH - 1) * STEP_Y + WW - 1
QR = 64
ROWS = 4 * QR
SPAN = 640
TABLE = 1280
GROUPS = Z * SH
LINES = Z * WH
LINE = 16
SCALE = HD ** (-0.5)
FAR = -1e30
VMEM_LIMIT = 58 * 1024 * 1024


def token_places():
    places = []
    for row in range(ROWS):
        quad, inner = divmod(row, QR)
        if inner >= GROUPS * SW:
            places.append(None)
            continue
        group, x = divmod(inner, SW)
        z, y = divmod(group, SH)
        places.append((z, y + SH * (quad // 2), x + SW * (quad % 2)))
    return places


def order_matrix():
    order = np.zeros((ROWS, LINES * LINE), np.float32)
    for row, place in enumerate(token_places()):
        if place is not None:
            z, y, x = place
            order[row, (z * WH + y) * LINE + x] = 1
    return order


def spread_matrix():
    spread = np.zeros((SPAN, ROWS), np.float32)
    for row, place in enumerate(token_places()):
        if place is not None:
            z, y, x = place
            spread[z * STEP_Z + y * STEP_Y + x, row] = 1
    return spread


def group_list():
    groups = []
    for quad in range(4):
        for group in range(GROUPS):
            z, y = divmod(group, SH)
            start = z * STEP_Z + (y + SH * (quad // 2)) * STEP_Y + SW * (quad % 2)
            groups.append((quad * QR + group * SW, CENTRE - start))
    return groups


def dot(a, b):
    return jnp.dot(a, b, preferred_element_type=jnp.float32)


def dot_t(a, b):
    return lax.dot_general(a, b, (((1,), (1,)), ((), ())), preferred_element_type=jnp.float32)


def t_dot(a, b):
    return lax.dot_general(a, b, (((0,), (0,)), ((), ())), preferred_element_type=jnp.float32)


STAGES = (5, 11, 2 * H)


def prep_stage(stage, tok, cot, tab, order, spread, x_out, g_out, bias_one, bias_two, lines, rows):
    if stage == 0:
        lines[...] = jnp.zeros_like(lines)
        for source, target in ((tok, x_out), (cot, g_out)):
            for k in range(LINES):
                lines[k, 0:WW, :] = source[k // WH, k % WH]
            flat = lines[...].reshape(LINES * LINE, lines.shape[2])
            target[...] = dot(order[...], flat).astype(jnp.bfloat16)
        rows[...] = jnp.zeros_like(rows)
    key = lax.broadcasted_iota(jnp.int32, (ROWS, ROWS), 1)
    query = lax.broadcasted_iota(jnp.int32, (ROWS, ROWS), 0)
    pad = key % QR >= GROUPS * SW
    polar = jnp.where(lax.axis_index("lat") == lax.axis_size("lat") - 1, 1, 0)
    apart = jnp.where((key // (2 * QR)) != (query // (2 * QR)), polar, 0)
    drops = (pad, pad | (apart == 1))

    def one_head(block, target, n, carry):
        base = jnp.broadcast_to(tab[block * H + n], (8, TABLE))
        base = pltpu.roll(base, 0, 1, stride=1, stride_axis=0)
        for row, shift in group_list():
            rows[row : row + SW, :] = pltpu.roll(base, TABLE - shift, 1)[:SW, :SPAN]
        wide = rows[...]
        high = wide.astype(jnp.bfloat16)
        rest = wide - high.astype(jnp.float32)
        mid = rest.astype(jnp.bfloat16)
        low = (rest - mid.astype(jnp.float32)).astype(jnp.bfloat16)
        part = spread[...]
        bias = dot(high, part) + dot(mid, part) + dot(low, part)
        target[n] = jnp.where(drops[block], FAR, bias)
        return carry

    first = 0 if stage == 0 else STAGES[stage - 1]
    last = STAGES[stage]
    for block, target in ((0, bias_one), (1, bias_two)):
        low, high = max(first - block * H, 0), min(last - block * H, H)
        if low < high:
            lax.fori_loop(low, high, functools.partial(one_head, block, target), 0)


def prep_kernel(*refs):
    for stage in range(len(STAGES)):
        prep_stage(stage, *refs)


def normalise(values):
    centred = values - jnp.mean(values, -1, keepdims=True)
    inverse = lax.rsqrt(jnp.mean(centred * centred, -1, keepdims=True) + EPS)
    return centred * inverse, inverse


def half_mask(which):
    lane = lax.broadcasted_iota(jnp.int32, (ROWS, 2 * HD), 1)
    return (lane // HD) == which


def forward_kernel(x_ref, gain, w_in, w_proj, bias, y_out, qkv, probs, ctx):
    normed, _ = normalise(x_ref[...].astype(jnp.float32))
    qkv[...] = dot((normed * gain[...]).astype(jnp.bfloat16), w_in[...]).astype(jnp.bfloat16)
    first_half = half_mask(0)
    for pair in range(H // 2):
        lo, hi = pair * 2 * HD, (pair + 1) * 2 * HD
        query = qkv[:, lo:hi] * jnp.bfloat16(SCALE)
        keys = qkv[:, H * HD + lo : H * HD + hi]
        values = qkv[:, 2 * H * HD + lo : 2 * H * HD + hi]
        found = []
        for side in range(2):
            keep = first_half if side == 0 else ~first_half
            scores = dot_t(jnp.where(keep, query, 0), keys) + bias[2 * pair + side]
            powers = jnp.exp(scores - jnp.max(scores, -1, keepdims=True))
            weights = (powers / jnp.sum(powers, -1, keepdims=True)).astype(jnp.bfloat16)
            probs[2 * pair + side] = weights
            found.append(dot(weights, values))
        ctx[:, lo:hi] = jnp.where(first_half, found[0], found[1]).astype(jnp.bfloat16)
    y_out[...] = (x_ref[...].astype(jnp.float32) + dot(ctx[...], w_proj[...])).astype(jnp.bfloat16)


def backward_core(g_ref, x_ref, gain, w_in, w_proj, qkv, probs, collect, gain_out, table_out,
                  gctx, gqkv, wide):
    gctx[...] = dot_t(g_ref[...], w_proj[...]).astype(jnp.bfloat16)
    first_half = half_mask(0)
    row_in_group = lax.broadcasted_iota(jnp.int32, (8, SPAN), 0) < SW
    zeros = jnp.zeros((8, TABLE - SPAN), jnp.float32)
    for pair in range(H // 2):
        lo, hi = pair * 2 * HD, (pair + 1) * 2 * HD
        query = qkv[:, lo:hi]
        keys = qkv[:, H * HD + lo : H * HD + hi]
        values = qkv[:, 2 * H * HD + lo : 2 * H * HD + hi]
        part = gctx[:, lo:hi]
        grads = []
        for side in range(2):
            head = 2 * pair + side
            keep = first_half if side == 0 else ~first_half
            weights_bf = probs[head]
            weights = weights_bf.astype(jnp.float32)
            grad_probs = dot_t(jnp.where(keep, part, 0), values)
            grad_scores = weights * (
                grad_probs - jnp.sum(grad_probs * weights, -1, keepdims=True)
            )
            s = grad_scores.astype(jnp.bfloat16)
            rest = (grad_scores - s.astype(jnp.float32)).astype(jnp.bfloat16)
            wide[head] = dot(s, collect[...]) + dot(rest, collect[...])
            grads.append((dot(s, keys), t_dot(s, query), t_dot(weights_bf, part)))
        for which, factor in ((0, SCALE), (1, SCALE), (2, 1.0)):
            both = jnp.where(first_half, grads[0][which], grads[1][which]) * factor
            at = which * H * HD
            gqkv[:, at + lo : at + hi] = both.astype(jnp.bfloat16)

    def fold(head, carry):
        total = jnp.zeros((8, TABLE), jnp.float32)
        for row, shift in group_list():
            rows = jnp.where(row_in_group, wide[head, row : row + 8, :], 0.0)
            total = total + pltpu.roll(jnp.concatenate([rows, zeros], 1), shift, 1)
        line = total[0:1]
        for x in range(1, SW):
            line = line + pltpu.roll(total[x : x + 1], TABLE - x, 1)
        table_out[head] = line
        return carry

    lax.fori_loop(0, H, fold, 0)
    grad_u = dot_t(gqkv[...], w_in[...])
    normed, inverse = normalise(x_ref[...].astype(jnp.float32))
    gain_out[...] = jnp.sum(grad_u * normed, 0, keepdims=True)
    scaled = grad_u * gain[...]
    return g_ref[...].astype(jnp.float32) + inverse * (
        scaled
        - jnp.mean(scaled, -1, keepdims=True)
        - normed * jnp.mean(scaled * normed, -1, keepdims=True)
    )


def backward_kernel(g_ref, x_ref, gain, w_in, w_proj, qkv, probs, collect,
                    gx_out, gain_out, table_out, gctx, gqkv, wide):
    grad = backward_core(g_ref, x_ref, gain, w_in, w_proj, qkv, probs, collect, gain_out,
                         table_out, gctx, gqkv, wide)
    gx_out[...] = grad.astype(jnp.bfloat16)


def last_kernel(g_ref, x_ref, gain, w_in, w_proj, qkv, probs, collect, y_ref, order,
                gx_out, gain_out, table_out, y_out, gctx, gqkv, wide):
    grad = backward_core(g_ref, x_ref, gain, w_in, w_proj, qkv, probs, collect, gain_out,
                         table_out, gctx, gqkv, wide)
    for source, target in ((grad.astype(jnp.bfloat16), gx_out), (y_ref[...], y_out)):
        lines = t_dot(order[...], source).astype(jnp.bfloat16)
        for k in range(LINES):
            target[k // WH, k % WH] = lines[k * LINE : k * LINE + WW]


def quad_target(quad, ahead, sign):
    lat, lon = lax.axis_index("lat"), lax.axis_index("lon")
    lats, lons = lax.axis_size("lat"), lax.axis_size("lon")
    y, x = quad // 2, quad % 2
    dy, dx = (1 - y, 1 - x) if ahead else (y, x)
    return {
        "lat": lax.rem(lat + lats + sign * dy, lats),
        "lon": lax.rem(lon + lons + sign * dx, lons),
    }


def exchange_kernel(ahead, src, dst, send, recv, own):
    sign = -1 if ahead else 1
    moving = [quad for quad in range(4) if quad != (3 if ahead else 0)]
    barrier = pltpu.get_barrier_semaphore()
    for quad in moving:
        pl.semaphore_signal(barrier, inc=1, device_id=quad_target(quad, ahead, -sign), device_id_type=MESH)
    stay = 3 if ahead else 0
    local = pltpu.make_async_copy(src.at[stay], dst.at[3 - stay], own)
    local.start()
    pl.semaphore_wait(barrier, 3)
    copies = []
    for n, quad in enumerate(moving):
        copies.append(
            pltpu.make_async_remote_copy(
                src_ref=src.at[quad],
                dst_ref=dst.at[3 - quad],
                send_sem=send.at[n],
                recv_sem=recv.at[n],
                device_id=quad_target(quad, ahead, sign),
                device_id_type=MESH,
            )
        )
        copies[-1].start()
    local.wait()
    for copy in copies:
        copy.wait()


def exchange(field, ahead, number):
    quads = field.reshape(4, QR, field.shape[-1])
    moved = pl.pallas_call(
        functools.partial(exchange_kernel, ahead),
        out_shape=jax.ShapeDtypeStruct(quads.shape, quads.dtype),
        in_specs=[pl.BlockSpec(memory_space=pltpu.VMEM)],
        out_specs=pl.BlockSpec(memory_space=pltpu.VMEM),
        scratch_shapes=[
            pltpu.SemaphoreType.DMA((3,)),
            pltpu.SemaphoreType.DMA((3,)),
            pltpu.SemaphoreType.DMA,
        ],
        compiler_params=pltpu.CompilerParams(collective_id=number, has_side_effects=True),
    )(quads)
    return moved.reshape(field.shape)


def call(kernel, out, scratch, args, smem=(), flops=10**9):
    specs = [
        pl.BlockSpec(memory_space=pltpu.SMEM if n in smem else pltpu.VMEM)
        for n in range(len(args))
    ]
    return pl.pallas_call(
        kernel,
        out_shape=[jax.ShapeDtypeStruct(shape, dtype) for shape, dtype in out],
        in_specs=specs,
        out_specs=[pl.BlockSpec(memory_space=pltpu.VMEM) for _ in out],
        scratch_shapes=[pltpu.VMEM(shape, dtype) for shape, dtype in scratch],
        compiler_params=pltpu.CompilerParams(vmem_limit_bytes=VMEM_LIMIT),
        cost_estimate=pl.CostEstimate(flops=flops, bytes_accessed=8 * 2**20, transcendentals=0),
    )(*args)


def shift_quads(field, ahead):
    lats, lons = lax.axis_size("lat"), lax.axis_size("lon")
    quads = field.reshape(4, QR, field.shape[-1])
    sign = -1 if ahead else 1
    arrived = []
    for slot in range(4):
        quad = 3 - slot
        y, x = quad // 2, quad % 2
        dy, dx = (1 - y, 1 - x) if ahead else (y, x)
        if dy == 0 and dx == 0:
            arrived.append(quads[quad])
            continue
        pairs = []
        for lat in range(lats):
            for lon in range(lons):
                target = ((lat + sign * dy) % lats) * lons + (lon + sign * dx) % lons
                pairs.append((lat * lons + lon, target))
        arrived.append(lax.ppermute(quads[quad], ("lat", "lon"), pairs))
    return jnp.concatenate(arrived, 0)


def peers_of(axis):
    me, size = lax.axis_index(axis), lax.axis_size(axis)
    ahead = [(d, lax.rem(me + d, size)) for d in range(1, size)]
    behind = [(d, lax.rem(me + size - d, size)) for d in range(1, size)]
    return me, ahead, behind


def gather_kernel(w_in, w_proj, tok, cot, tab, order, spread, in_one, in_two, proj_one, proj_two,
                  x_out, g_two, bias_one, bias_two, g_out, lines, rows, send_z, recv_z, send_p,
                  recv_p, send_c, recv_c, send_g, recv_g, own):
    prep = functools.partial(prep_stage, tok=tok, cot=cot, tab=tab, order=order, spread=spread,
                             x_out=x_out, g_out=g_out, bias_one=bias_one, bias_two=bias_two,
                             lines=lines, rows=rows)
    dp, dp_ahead, _ = peers_of("dp")
    lat, lat_ahead, _ = peers_of("lat")
    lon, lon_ahead, lon_behind = peers_of("lon")
    lons = lax.axis_size("lon")
    arrays = (
        (w_in.at[0], in_one), (w_proj.at[0], proj_one),
        (w_in.at[1], in_two), (w_proj.at[1], proj_two),
    )
    mine = lat * lons + lon
    barrier = pltpu.get_barrier_semaphore()
    friends = [{"dp": peer} for _, peer in dp_ahead] + [{"lat": peer} for _, peer in lat_ahead]
    friends += [{"lon": peer} for _, peer in lon_ahead]
    friends += [quad_target(quad, True, 1) for quad in range(3)]
    for friend in friends:
        pl.semaphore_signal(barrier, inc=1, device_id=friend, device_id_type=MESH)
    pl.semaphore_wait(barrier, len(friends))
    sent = []

    def put(src, dst, send, recv, device):
        copy = pltpu.make_async_remote_copy(
            src_ref=src, dst_ref=dst, send_sem=send, recv_sem=recv, device_id=device,
            device_id_type=MESH,
        )
        copy.start()
        sent.append(copy)
        return copy

    along = {}
    for d, peer in lon_ahead:
        for n, (part, full) in enumerate(arrays):
            along[d, n] = put(part.at[dp], full.at[mine, dp], send_z.at[n, d], recv_z.at[n, d],
                              {"lon": peer})
    local = []
    across = []
    for n, (part, full) in enumerate(arrays):
        local.append(pltpu.make_async_copy(part, full.at[mine], own.at[n]))
        local[-1].start()
        for f, peer in lat_ahead:
            across.append(put(part, full.at[mine], send_c.at[n, 0, f], recv_c.at[n, 0, f],
                              {"lat": peer}))
    prep(0)
    g_two[0:QR] = g_out[3 * QR : 4 * QR]
    rolled = [
        put(g_out.at[pl.ds(quad * QR, QR)], g_two.at[pl.ds((3 - quad) * QR, QR)], send_g.at[quad],
            recv_g.at[quad], quad_target(quad, True, -1))
        for quad in range(3)
    ]
    plane = {}
    for d, source in lon_behind:
        shard = lat * lons + source
        for n, (_, full) in enumerate(arrays):
            along[d, n].wait_recv()
            for e, peer in dp_ahead:
                plane[d, n, e] = put(full.at[shard, dp], full.at[shard, dp], send_p.at[n, d, e],
                                     recv_p.at[n, d, e], {"dp": peer})
    prep(1)
    for d, source in lon_behind:
        shard = lat * lons + source
        for n, (_, full) in enumerate(arrays):
            for e, _ in dp_ahead:
                plane[d, n, e].wait_recv()
            for f, peer in lat_ahead:
                across.append(put(full.at[shard], full.at[shard], send_c.at[n, d, f],
                                  recv_c.at[n, d, f], {"lat": peer}))
    prep(2)
    for copy in local:
        copy.wait()
    for copy in across + rolled:
        copy.wait_recv()
    for copy in sent:
        copy.wait_send()


def fetch_all(w_qkv, w_out, prep_args, prep_out, prep_scratch):
    dps, lats, lons = (lax.axis_size(axis) for axis in ("dp", "lat", "lon"))
    shards = lats * lons
    if w_qkv.shape[1] % (16 * dps) or w_out.shape[1] % (16 * dps):
        one, two = fetch_block(w_qkv, w_out, 0), fetch_block(w_qkv, w_out, 1)
        x_one, g_out, bias_one, bias_two = call(
            prep_kernel, prep_out, prep_scratch, prep_args, flops=8 * 10**9
        )
        return (one[0], two[0], one[1], two[1]), (
            x_one, shift_quads(g_out, True), bias_one, bias_two
        )
    parts = [w.reshape(2, dps, w.shape[1] // dps, w.shape[2]) for w in (w_qkv, w_out)]
    dma = pltpu.SemaphoreType.DMA
    shapes = [((shards,) + part.shape[1:], part.dtype) for part in parts for _ in range(2)]
    vmem = pl.BlockSpec(memory_space=pltpu.VMEM)
    shapes = shapes + prep_out
    found = pl.pallas_call(
        gather_kernel,
        out_shape=[jax.ShapeDtypeStruct(shape, dtype) for shape, dtype in shapes],
        in_specs=[vmem] * (2 + len(prep_args)),
        out_specs=[vmem] * len(shapes),
        scratch_shapes=[pltpu.VMEM(shape, dtype) for shape, dtype in prep_out[1:2] + prep_scratch]
        + [
            dma((4, lons)), dma((4, lons)), dma((4, lons, dps)), dma((4, lons, dps)),
            dma((4, lons, lats)), dma((4, lons, lats)), dma((3,)), dma((3,)), dma((4,)),
        ],
        compiler_params=pltpu.CompilerParams(
            collective_id=5, has_side_effects=True, vmem_limit_bytes=VMEM_LIMIT
        ),
    )(*parts, *prep_args)
    return tuple(array.reshape(-1, array.shape[-1]) for array in found[:4]), found[4:]


def plane_peers():
    dps, lats = lax.axis_size("dp"), lax.axis_size("lat")
    dp, lat = lax.axis_index("dp"), lax.axis_index("lat")
    ahead, behind = [], []
    for far in range(1, dps * lats):
        a, b = far // dps, far % dps
        ahead.append((far, lax.rem(lat + a, lats), lax.rem(dp + b, dps)))
        behind.append((far, lax.rem(lat + lats - a, lats), lax.rem(dp + dps - b, dps)))
    return ahead, behind


def reduce_kernel(data, total, from_plane, from_lon, send, recv, send_z, recv_z):
    dp, lat = lax.axis_index("dp"), lax.axis_index("lat")
    ahead, behind = plane_peers()
    lon, lon_ahead, _ = peers_of("lon")
    lons = lax.axis_size("lon")
    barrier = pltpu.get_barrier_semaphore()
    for _, a, b in ahead:
        pl.semaphore_signal(
            barrier, inc=1, device_id={"lat": a, "dp": b}, device_id_type=MESH
        )
    for _, peer in lon_ahead:
        pl.semaphore_signal(barrier, inc=1, device_id={"lon": peer}, device_id_type=MESH)
    pl.semaphore_wait(barrier, len(ahead) + len(lon_ahead))
    sent = []

    def put(src, dst, send_sem, recv_sem, device):
        copy = pltpu.make_async_remote_copy(
            src_ref=src, dst_ref=dst, send_sem=send_sem, recv_sem=recv_sem, device_id=device,
            device_id_type=MESH,
        )
        copy.start()
        sent.append(copy)
        return copy

    first = [
        put(data.at[a, b], from_plane.at[lat, dp], send.at[0, d], recv.at[0, d],
            {"lat": a, "dp": b})
        for d, a, b in ahead
    ]
    value = data[lat, dp]
    for copy in first:
        copy.wait_recv()
    for _, a, b in behind:
        value = value + from_plane[a, b]
    from_lon[lon] = value
    second = [
        put(from_lon.at[lon], from_lon.at[lon], send_z.at[d], recv_z.at[d], {"lon": peer})
        for d, peer in lon_ahead
    ]
    for copy in second:
        copy.wait_recv()
    value = from_lon[0]
    for n in range(1, lons):
        value = value + from_lon[n]
    total[lat, dp] = value
    third = [
        put(total.at[lat, dp], total.at[lat, dp], send.at[1, d], recv.at[1, d],
            {"lat": a, "dp": b})
        for d, a, b in ahead
    ]
    for copy in third:
        copy.wait_recv()
    for copy in sent:
        copy.wait_send()


def sum_all(packed):
    dps, lats, lons = (lax.axis_size(axis) for axis in ("dp", "lat", "lon"))
    length = packed.shape[1]
    rows = -(-length // (128 * 8 * dps * lats)) * 8
    padded = jnp.pad(packed[0], (0, rows * 128 * dps * lats - length))
    f32 = jnp.float32
    piece = (rows, 128)
    total = pl.pallas_call(
        reduce_kernel,
        out_shape=jax.ShapeDtypeStruct((lats, dps) + piece, f32),
        in_specs=[pl.BlockSpec(memory_space=pltpu.VMEM)],
        out_specs=pl.BlockSpec(memory_space=pltpu.VMEM),
        scratch_shapes=[
            pltpu.VMEM((lats, dps) + piece, f32),
            pltpu.VMEM((lons,) + piece, f32),
            pltpu.SemaphoreType.DMA((2, dps * lats)),
            pltpu.SemaphoreType.DMA((2, dps * lats)),
            pltpu.SemaphoreType.DMA((lons,)),
            pltpu.SemaphoreType.DMA((lons,)),
        ],
        compiler_params=pltpu.CompilerParams(collective_id=6, has_side_effects=True),
    )(padded.reshape((lats, dps) + piece))
    return total.reshape(1, -1)[:, :length]


def fetch_block(w_qkv, w_out, index):
    return (
        lax.all_gather(w_qkv[index], ("lat", "lon"), axis=0, tiled=True),
        lax.all_gather(w_out[index], ("lat", "lon"), axis=0, tiled=True),
    )


def on_device(tokens, cotangent, w_qkv, w_out, gains, tables):
    features = tokens.shape[-1]
    bf, f32 = jnp.bfloat16, jnp.float32
    inner = H * HD
    order = jnp.asarray(order_matrix(), bf)
    spread = jnp.asarray(spread_matrix(), bf)
    collect = jnp.asarray(spread_matrix().T.copy(), bf)
    lines = jnp.pad(tables.reshape(2 * H, 1, RELS)[:, :, ::-1], ((0, 0), (0, 0), (0, TABLE - RELS)))
    field = ((ROWS, features), bf)
    bias = ((H, ROWS, ROWS), f32)
    (in_one, in_two, proj_one, proj_two), (x_one, g_two, bias_one, bias_two) = fetch_all(
        w_qkv,
        w_out,
        (tokens[0], cotangent[0], lines, order, spread),
        [field, field, bias, bias],
        [((LINES, LINE, features), bf), ((ROWS, SPAN), f32)],
    )
    saved = [((ROWS, 3 * inner), bf), ((H, ROWS, ROWS), bf)]
    wide = [((ROWS, inner), bf)]
    gain_one, gain_two = gains[0:1], gains[1:2]
    first, qkv_one, probs_one = call(
        forward_kernel, [field] + saved, wide, (x_one, gain_one, in_one, proj_one, bias_one)
    )
    x_two = exchange(first, True, 1)
    second, qkv_two, probs_two = call(
        forward_kernel, [field] + saved, wide, (x_two, gain_two, in_two, proj_two, bias_two)
    )
    y_back = shift_quads(second, False)
    back = [((ROWS, inner), bf), ((ROWS, 3 * inner), bf), ((H, ROWS, SPAN), f32)]
    terms = [((1, features), f32), ((H, 1, TABLE), f32)]
    gx_two, gterm_two, tterm_two = call(
        backward_kernel,
        [field] + terms,
        back,
        (g_two, x_two, gain_two, in_two, proj_two, qkv_two, probs_two, collect),
    )
    g_one = exchange(gx_two, False, 3)
    window = (tokens.shape[1:], bf)
    grad_tokens, gterm_one, tterm_one, outputs = call(
        last_kernel,
        [window] + terms + [window],
        back,
        (g_one, x_one, gain_one, in_one, proj_one, qkv_one, probs_one, collect, y_back, order),
    )
    packed = jnp.concatenate(
        [gterm_one, gterm_two, tterm_one.reshape(1, -1), tterm_two.reshape(1, -1)], 1
    )
    packed = sum_all(packed)
    total = math.prod(tokens.shape[:4]) * math.prod(
        lax.axis_size(axis) for axis in ("dp", "lat", "lon")
    )
    packed = packed * (1.0 / math.sqrt(total))
    grad_gains = packed[:, : 2 * features].reshape(2, features)
    folded = packed[:, 2 * features :].reshape(2, H, TABLE)
    grad_tables = folded[:, :, :RELS][:, :, ::-1]
    return (outputs[None], grad_tokens[None], grad_gains, grad_tables)


def solution(mesh):
    return jax.shard_map(
        on_device,
        mesh=mesh,
        in_specs=(
            P("dp", None, "lat", "lon", None),
            P("dp", None, "lat", "lon", None),
            P(None, ("lat", "lon"), None),
            P(None, ("lat", "lon"), None),
            P(),
            P(),
        ),
        out_specs=(P("dp", None, "lat", "lon", None), P("dp", None, "lat", "lon", None), P(), P()),
        check_vma=False,
    )
```
